256 devices in a mesh: pipe: 16 (over x, y), expert: 16 (over z, core).
Axes of the slice: x: 4, y: 4, z: 8, core: 2. Of those that a mesh axis runs over, the one named last changes fastest.
Arguments:
- fwd_acts: bfloat16 [16, 1024, 3584], P('pipe', 'expert'), may hold values from -6 to 6
- fwd_route: int32 [16, 1024, 1], P('pipe', 'expert'), may hold values from 0 to 3; in each aligned block of 64 rows (0 to 63, 64 to 127, ..., all dimensions but the last counted through in order) at most 24 rows name the same one
- fwd_gate: float32 [16, 1024, 1], P('pipe', 'expert'), may hold values from 0.1 to 1
- saved_x: bfloat16 [16, 1024, 3584], P('pipe', 'expert'), may hold values from -6 to 6
- bwd_grads: bfloat16 [16, 1024, 3584], P('pipe', 'expert'), may hold values from -6 to 6
- bwd_route: int32 [16, 1024, 1], P('pipe', 'expert'), may hold values from 0 to 3; in each aligned block of 64 rows (0 to 63, 64 to 127, ..., all dimensions but the last counted through in order) at most 24 rows name the same one
- bwd_gate: float32 [16, 1024, 1], P('pipe', 'expert'), may hold values from 0.1 to 1
- w_gate: bfloat16 [16, 3584, 8192], P('pipe', None, 'expert'), may hold values from -0.09375 to 0.09375
- w_up: bfloat16 [16, 3584, 8192], P('pipe', None, 'expert'), may hold values from -0.09375 to 0.09375
- w_down: bfloat16 [16, 8192, 3584], P('pipe', 'expert'), may hold values from -0.125 to 0.125
Outputs:
- fwd_out: bfloat16 [16, 1024, 3584], P('pipe', 'expert')
- grad_out: bfloat16 [16, 1024, 3584], P('pipe', 'expert')
The draws below stay inside these ranges and needn't reach their ends.
Inputs may be any that keep to these rules, and one draw needn't show every extreme that they name: `fwd_route`: in each aligned block of 64 rows (the rows of one device) no expert is named by more than 24 rows, a bound that some block reaches. `bwd_route`: in each aligned block of 64 rows (the rows of one device) no expert is named by more than 24 rows, a bound that some block reaches.
All inputs are finite; a program needn't handle non-finite values.
Results may differ from the reference program's by a relative error of at most 0.0039.
Values may be sent and summed in bfloat16 or wider, within the bound.
A program may use at most 128 MiB of HBM per device.

```python
import math
import jax
import jax.numpy as jnp
import numpy as np
from jax import lax

D = 3584
HIDDEN_SIZE = 2048
EXP_SECTION = 4
TOPK = 1
TOK_DEV = 64
MOST = 24
SPLIT = 4
HID_DEV = 512
TOKENS = 1024
SECTIONS = 16
N_EXPERT = 16


def levels(own_key, extent, cuts, low, largest):
    loudness = 1.0
    for position, parts in cuts:
        heights = jax.random.uniform(jax.random.fold_in(jax.random.fold_in(own_key, 6), position), (parts,), jnp.float32, low / len(cuts), largest / len(cuts))
        loudness = loudness * jnp.repeat(jnp.exp(heights), extent[position] // parts).reshape((-1,) + (1,) * (len(extent) - 1 - position))
    return loudness


def routed_block(stream_key, own, number, rows, amount, top, bound, lean):
    ranking = jax.random.permutation(stream_key, amount)
    heavy_load, ordinary = shares(amount, rows * top, bound, lean, True), shares(amount, rows * top, bound, lean, False)
    places = jnp.arange(amount)

    def named(tallies, turn):
        used = int((tallies > 0).sum())
        fixed = max(1, used // 4)
        shifted = fixed + (places - fixed + turn * (used - fixed)) % max(1, amount - fixed)
        return jnp.zeros((amount,), jnp.int32).at[ranking[jnp.where(places < fixed, places, shifted)]].set(jnp.asarray(tallies, jnp.int32))

    tallies = jnp.where(number % 4 == 0, named(heavy_load, number // 4), named(ordinary, number - number // 4 - 1))
    mixed = jax.random.permutation(jax.random.fold_in(own, 3), amount)
    donor, sink = mixed[0:amount // 2 * 2:2], mixed[1:amount // 2 * 2:2]
    slack = jnp.minimum(tallies[donor] - 1, bound - tallies[sink]) // 2
    slack = jnp.where((donor == ranking[0]) | (sink == ranking[0]) | (tallies[sink] == 0), 0, jnp.maximum(slack, 0))
    shifted = jax.random.randint(jax.random.fold_in(own, 4), (amount // 2,), 0, 1 << 20) % (slack + 1)
    tallies = tallies.at[donor].add(-shifted).at[sink].add(shifted)
    members = jnp.searchsorted(jnp.cumsum(tallies), jnp.arange(rows * top), side="right").astype(jnp.int32)
    listing = members.reshape(top, rows).T
    listing = listing[jax.random.permutation(jax.random.fold_in(own, 1), rows)]
    turn = jax.random.randint(jax.random.fold_in(own, 2), (rows, 1), 0, top)
    return jnp.take_along_axis(listing, (jnp.arange(top)[None, :] + turn) % top, axis=1)


def shares(count, total, reach, lean, full):
    portions = [(1 << 20) // math.isqrt(rank ** lean) + 1 for rank in range(1, count + 1)]
    largest = reach if full else min(reach, max(-(-total // count), total * portions[0] // sum(portions)))
    least = 1 if total - largest >= count - 1 else 0
    counts, rest = [largest] + [least] * (count - 1), total - largest - least * (count - 1)
    while rest > 0:
        candidates = [i for i in range(1, count) if counts[i] < largest] or [i for i in range(1, count) if counts[i] < reach]
        whole, remaining = sum([portions[i] for i in candidates]), rest
        for i in candidates:
            more = min(reach - counts[i], max(1, remaining * portions[i] // whole), rest)
            counts[i] = counts[i] + more
            rest = rest - more
    return np.array(counts)


def normal_values(own_key, shape, spread, limit, split=(), dtype=jnp.bfloat16):
    entries = jax.random.normal(own_key, shape, jnp.float32) * spread
    if len(split) > 0:
        entries = levels(own_key, shape, split, -0.22, 0.18) * entries
    return jnp.clip(entries, min=-limit, max=limit).astype(dtype)


def setup_inputs(seed: int = 0) -> dict:
    key_of = jax.random.split(jax.random.key(seed), 11)
    fwd_acts = normal_values(key_of[0], (SECTIONS, TOKENS, D), 1.0, 6.0, ((0, 16), (1, 16)))
    fwd_route_keys = jax.random.split(jax.random.fold_in(key_of[1], 1), SECTIONS * TOKENS // TOK_DEV)
    fwd_route_turns = jax.random.permutation(jax.random.fold_in(key_of[1], 3), SECTIONS * TOKENS // TOK_DEV)
    fwd_route = jax.vmap(lambda own, number: routed_block(jax.random.fold_in(key_of[1], 2), own, number, TOK_DEV, EXP_SECTION, TOPK, MOST, 2))(fwd_route_keys, fwd_route_turns).reshape((SECTIONS, TOKENS, TOPK))
    fwd_gate = jnp.clip(0.1 + 0.9 * jax.random.uniform(key_of[2], (SECTIONS, TOKENS, TOPK), jnp.float32) ** levels(key_of[2], (SECTIONS, TOKENS, TOPK), ((0, 16), (1, 16)), -0.2, 0.2), 0.1, 1.0)
    saved_x = normal_values(key_of[3], (SECTIONS, TOKENS, D), 1.0, 6.0, ((0, 16), (1, 16)))
    bwd_grads = normal_values(key_of[4], (SECTIONS, TOKENS, D), 1.0, 6.0, ((0, 16), (1, 16)))
    bwd_route_keys = jax.random.split(jax.random.fold_in(key_of[5], 1), SECTIONS * TOKENS // TOK_DEV)
    bwd_route_turns = jax.random.permutation(jax.random.fold_in(key_of[5], 3), SECTIONS * TOKENS // TOK_DEV)
    bwd_route = jax.vmap(lambda own, number: routed_block(jax.random.fold_in(key_of[5], 2), own, number, TOK_DEV, EXP_SECTION, TOPK, MOST, 2))(bwd_route_keys, bwd_route_turns).reshape((SECTIONS, TOKENS, TOPK))
    bwd_gate = jnp.clip(0.1 + 0.9 * jax.random.uniform(key_of[6], (SECTIONS, TOKENS, TOPK), jnp.float32) ** levels(key_of[6], (SECTIONS, TOKENS, TOPK), ((0, 16), (1, 16)), -0.2, 0.2), 0.1, 1.0)
    w_gate = normal_values(key_of[7], (SECTIONS, D, EXP_SECTION * HIDDEN_SIZE), D ** -0.5, 0.09375, ((0, 16), (2, 16)))
    w_up = normal_values(key_of[8], (SECTIONS, D, EXP_SECTION * HIDDEN_SIZE), D ** -0.5, 0.09375, ((0, 16), (2, 16)))
    w_down = normal_values(key_of[9], (SECTIONS, EXP_SECTION * HIDDEN_SIZE, D), HIDDEN_SIZE ** -0.5, 0.125, ((0, 16), (1, 16)))
    return dict(fwd_acts=fwd_acts, fwd_route=fwd_route, fwd_gate=fwd_gate, saved_x=saved_x, bwd_grads=bwd_grads, bwd_route=bwd_route, bwd_gate=bwd_gate, w_gate=w_gate, w_up=w_up, w_down=w_down)


def round_trip(values):
    return lax.optimization_barrier(values.astype(jnp.bfloat16)).astype(jnp.float32)


def forward_rows(rows, gate_weight, up_weight, down_weight):
    gate_pre = jnp.dot(rows, gate_weight, preferred_element_type=jnp.float32)
    up_pre = jnp.dot(rows, up_weight, preferred_element_type=jnp.float32)
    active = (jax.nn.silu(gate_pre) * up_pre).astype(jnp.bfloat16)
    total = jnp.zeros((rows.shape[0], D), jnp.float32)
    for block in range(SPLIT):
        first = block * HID_DEV
        piece = jnp.dot(active[:, first:first + HID_DEV], down_weight[first:first + HID_DEV], preferred_element_type=jnp.float32)
        total = total + round_trip(piece)
    return total


def backward_rows(rows, upstream, gate_weight, up_weight, down_weight):
    contract = (((1,), (1,)), ((), ()))
    gate_pre = jnp.dot(rows, gate_weight, preferred_element_type=jnp.float32)
    up_pre = jnp.dot(rows, up_weight, preferred_element_type=jnp.float32)
    sigmoid_gate = jax.nn.sigmoid(gate_pre)
    hidden_grad = lax.dot_general(upstream, down_weight, contract, preferred_element_type=jnp.float32)
    grad_up = (hidden_grad * gate_pre * sigmoid_gate).astype(jnp.bfloat16)
    grad_gate = (hidden_grad * up_pre * sigmoid_gate * (1.0 + gate_pre * (1.0 - sigmoid_gate))).astype(jnp.bfloat16)
    total = jnp.zeros((rows.shape[0], D), jnp.float32)
    for block in range(SPLIT):
        first = block * HID_DEV
        last = first + HID_DEV
        piece = lax.dot_general(grad_gate[:, first:last], gate_weight[:, first:last], contract, preferred_element_type=jnp.float32)
        piece = piece + lax.dot_general(grad_up[:, first:last], up_weight[:, first:last], contract, preferred_element_type=jnp.float32)
        total = total + round_trip(piece)
    return total


def chosen_rows(route_column, expert):
    capacity = N_EXPERT * MOST
    found = jnp.nonzero(route_column == expert, size=capacity, fill_value=TOKENS)[0]
    return found.astype(jnp.int32)


def section_pass(packed):
    inputs, f_route, f_gate, saved, upstream, b_route, b_gate, gate_weight, up_weight, down_weight = packed
    mixed = jnp.zeros((TOKENS, D), jnp.float32)
    mixed_back = jnp.zeros((TOKENS, D), jnp.float32)
    for expert in range(EXP_SECTION):
        low = expert * HIDDEN_SIZE
        high = low + HIDDEN_SIZE
        gate_part = gate_weight[:, low:high]
        up_part = up_weight[:, low:high]
        down_part = down_weight[low:high]
        for choice_k in range(TOPK):
            places = chosen_rows(f_route[:, choice_k], expert)
            rows = jnp.take(inputs, places, axis=0, mode="fill", fill_value=0)
            weight = jnp.take(f_gate[:, choice_k], places, mode="fill", fill_value=0.0)
            result = forward_rows(rows, gate_part, up_part, down_part)
            mixed = mixed.at[places].add(result * weight[:, None], mode="drop")
            places = chosen_rows(b_route[:, choice_k], expert)
            rows = jnp.take(saved, places, axis=0, mode="fill", fill_value=0)
            grads = jnp.take(upstream, places, axis=0, mode="fill", fill_value=0)
            weight = jnp.take(b_gate[:, choice_k], places, mode="fill", fill_value=0.0)
            result = backward_rows(rows, grads, gate_part, up_part, down_part)
            mixed_back = mixed_back.at[places].add(result * weight[:, None], mode="drop")
    fwd_row = (inputs.astype(jnp.float32) + mixed).astype(jnp.bfloat16)
    grad_row = (upstream.astype(jnp.float32) + mixed_back).astype(jnp.bfloat16)
    return fwd_row, grad_row


def reference(fwd_acts, fwd_route, fwd_gate, saved_x, bwd_grads, bwd_route, bwd_gate, w_gate, w_up, w_down):
    inputs = jnp.roll(fwd_acts, 1, axis=0)
    upstream = jnp.roll(bwd_grads, -1, axis=0)
    fwd_out, grad_out = lax.map(section_pass, (inputs, fwd_route, fwd_gate, saved_x, upstream, bwd_route, bwd_gate, w_gate, w_up, w_down))
    return fwd_out, grad_out
```

```python
import functools

import jax
import jax.numpy as jnp
from jax import lax
from jax.experimental import pallas as pl
from jax.experimental.pallas import tpu as pltpu
from jax.sharding import PartitionSpec as P

D = 3584
HALF = D // 2
TOK = 64
HID = 512
MOST = 24
BLOCK = 2 * MOST
ROWS = 4 * BLOCK
TILE = 256
MESH = pl.DeviceIdType.MESH
F32 = jnp.float32
BF16 = jnp.bfloat16
NN = (((1,), (0,)), ((), ()))
NT = (((1,), (1,)), ((), ()))

N_SEM = 128


def dot(a, b, how=NN):
    return lax.dot_general(a, b, how, preferred_element_type=F32)


def kernel(
    acts,
    f_route,
    f_gate,
    saved,
    grads,
    b_route,
    b_gate,
    w_gate,
    w_up,
    w_down,
    f_out,
    b_out,
    wg,
    wu,
    wd,
    meta,
    f_place,
    b_place,
    f_pick,
    b_pick,
    tok_s,
    tok_g,
    tok_f,
    pk_s,
    pk_g,
    pk_f,
    rx_s,
    rx_g,
    rx_f,
    hid_a,
    hid_b,
    b_psend,
    b_precv,
    b_own,
    b_far,
    b_pr,
    b_home,
    b_ret,
    f_psend,
    f_precv,
    f_own,
    f_far,
    f_pr,
    f_home,
    f_ret,
    outs_send,
    outs_recv,
    send_sem,
    recv_sem,
    load_sem,
):
    sec = lax.axis_index("pipe")
    ex = lax.axis_index("expert")
    n_sec = lax.axis_size("pipe")
    n_ex = lax.axis_size("expert")
    z = lax.div(ex, 2)
    c = lax.rem(ex, 2)
    sgn = 1 - 2 * lax.rem(z, 2)
    pair = lax.div(z, 2)

    def along(dist):
        return (sec, lax.rem(ex + 2 * dist * sgn + 2 * n_ex, n_ex))

    other = (sec, ex + 1 - 2 * c)
    partner = along(1)
    target = {1: along(-1), 2: along(2), 3: along(-3)}
    source = {1: along(-1), 2: along(-2), 3: along(-3)}
    nxt = lax.rem(sec + 1, n_sec)
    prv = lax.rem(sec + n_sec - 1, n_sec)

    count = [0]
    pending = []

    def copy(src, dst, to, sem=None):
        i = count[0]
        count[0] += 1
        out = pltpu.make_async_remote_copy(
            src_ref=src,
            dst_ref=dst,
            send_sem=send_sem.at[i],
            recv_sem=recv_sem.at[i] if sem is None else recv_sem.at[sem],
            device_id=to,
            device_id_type=MESH,
        )
        pending.append(out)
        return out

    loads = [
        pltpu.make_async_copy(w_gate.at[0], wg, load_sem.at[0]),
        pltpu.make_async_copy(w_up.at[0], wu, load_sem.at[1]),
        pltpu.make_async_copy(w_down.at[0], wd, load_sem.at[2]),
    ]
    mine = pl.ds(pl.multiple_of(c * TOK, TOK), TOK)
    half_mine = pl.ds(pl.multiple_of(c * HALF, HALF), HALF)
    half_other = pl.ds(pl.multiple_of((1 - c) * HALF, HALF), HALF)
    own_saved = pltpu.make_async_copy(
        saved.at[0, :, half_mine], tok_s.at[mine], load_sem.at[3]
    )
    own_saved.start()

    barrier = pltpu.get_barrier_semaphore()
    friends = [
        other,
        partner,
        along(-1),
        along(2),
        along(-2),
        along(-3),
        (nxt, 2 * z),
        (nxt, 2 * z + 1),
        (prv, 2 * z),
        (prv, 2 * z + 1),
    ]
    for friend in friends:
        pl.semaphore_signal(barrier, inc=1, device_id=friend, device_id_type=MESH)
    for load in loads:
        load.start()

    lane = lax.broadcasted_iota(jnp.int32, (TOK, 128), 1)
    row = lax.broadcasted_iota(jnp.int32, (TOK, TOK), 0)
    col = lax.broadcasted_iota(jnp.int32, (TOK, TOK), 1)
    below = jnp.where(col < row, 1.0, 0.0).astype(BF16)
    for which, (route, gate) in enumerate(((f_route, f_gate), (b_route, b_gate))):
        named = jnp.broadcast_to(route[0], (TOK, 128))
        turn = lax.rem((named - pair) * sgn + 8, 4)
        near = jnp.where(turn == 0, 0, jnp.where(turn == 1, 2, jnp.where(turn == 2, 3, 1)))
        hot = jnp.where(near == lane, 1.0, 0.0)
        before = dot(below, hot.astype(BF16))
        rank = jnp.sum(hot * before, axis=1, keepdims=True)
        slot = (near * BLOCK + c * MOST).astype(F32) + rank
        meta[mine, which * 128 : which * 128 + 128] = slot
        meta[mine, 256 + which * 128 : 384 + which * 128] = jnp.broadcast_to(gate[0], (TOK, 128))
    f_ret[ROWS:, :] = jnp.zeros((256 - ROWS, HALF), BF16)
    b_ret[ROWS:, :] = jnp.zeros((256 - ROWS, HALF), BF16)

    pl.semaphore_wait(barrier, len(friends))

    swap_meta = copy(meta.at[mine], meta.at[mine], other)
    swap_meta.start()
    swap_saved = copy(saved.at[0, :, half_other], tok_s.at[mine], other)
    swap_saved.start()

    def relay_pipe(tokens, land, to_sec):
        base = count[0]
        for half in range(2):
            cp = copy(
                tokens.at[0, :, half * HALF : half * HALF + HALF],
                land.at[mine],
                (to_sec, 2 * z + half),
                sem=base + c,
            )
            cp.start()

        def wait():
            for src in range(2):
                pltpu.make_async_remote_copy(
                    src_ref=tokens.at[0, :, 0:HALF],
                    dst_ref=land.at[src * TOK : src * TOK + TOK],
                    send_sem=send_sem.at[base],
                    recv_sem=recv_sem.at[base + src],
                    device_id=other,
                    device_id_type=MESH,
                ).wait_recv()

        return wait

    wait_g = relay_pipe(grads, tok_g, prv)
    wait_f = relay_pipe(acts, tok_f, nxt)

    swap_meta.wait_recv()
    lanes = lax.broadcasted_iota(jnp.int32, (2 * TOK, 128), 1).astype(F32)
    for which, (place, pick) in enumerate(((f_place, f_pick), (b_place, b_pick))):
        slot = meta[:, which * 128 : which * 128 + 128]
        hot = jnp.concatenate(
            [jnp.where(slot == lanes, 1.0, 0.0), jnp.where(slot == lanes + 128.0, 1.0, 0.0)], axis=1
        )
        pick[...] = hot.astype(BF16)
        place[...] = hot.T.astype(BF16)

    def rows(k, n=1):
        return slice(k * BLOCK, (k + n) * BLOCK)

    class Dispatch:
        def __init__(self, tok, place, pk, rx):
            self.tok, self.place, self.pk, self.rx = tok, place, pk, rx
            self.near, self.over, self.cross = {}, {}, {}

        def send(self):
            for j in range(0, HALF, TILE):
                self.pk[:, j : j + TILE] = dot(
                    self.place[0:ROWS, :], self.tok[:, j : j + TILE]
                ).astype(BF16)
            for k in (3, 2, 1):
                self.near[k] = copy(self.pk.at[rows(k)], self.rx.at[c, rows(k)], target[k])
                self.near[k].start()
            self.rx[c, rows(0)] = self.pk[rows(0)]
            self.relay(0)

        def relay(self, k):
            if k:
                self.near[k].wait_recv()
            here = self.rx.at[c, rows(k)]
            self.over[k] = copy(here, self.rx.at[c, rows(4 + k)], partner)
            self.over[k].start()
            self.cross[k] = copy(here, here, other)
            self.cross[k].start()

        def hand(self, k):
            self.over[k].wait_recv()
            here = self.rx.at[c, rows(4 + k)]
            self.cross[4 + k] = copy(here, here, other)
            self.cross[4 + k].start()

        def ready(self, ks):
            for k in ks:
                self.cross[k].wait_recv()

    ds = Dispatch(tok_s, b_place, pk_s, rx_s)
    dg = Dispatch(tok_g, b_place, pk_g, rx_g)
    df = Dispatch(tok_f, f_place, pk_f, rx_f)

    def x_of(ref, chunk):
        first = chunk * ROWS
        return ref[0, first : first + ROWS, :], ref[1, first : first + ROWS, :]

    def hidden_bwd(chunk):
        @pl.loop(0, HID // TILE)
        def _(n):
            cols = pl.ds(pl.multiple_of(n * TILE, TILE), TILE)
            x0, x1 = x_of(rx_s, chunk)
            pre = dot(x0, wg[0:HALF, cols]) + dot(x1, wg[HALF:D, cols])
            up = dot(x0, wu[0:HALF, cols]) + dot(x1, wu[HALF:D, cols])
            g0, g1 = x_of(rx_g, chunk)
            back = dot(g0, wd[cols, 0:HALF], NT) + dot(g1, wd[cols, HALF:D], NT)
            sig = lax.logistic(pre)
            hid_b[:, cols] = (back * pre * sig).astype(BF16)
            hid_a[:, cols] = (back * up * sig * (1.0 + pre * (1.0 - sig))).astype(BF16)

    def hidden_fwd(chunk):
        @pl.loop(0, HID // TILE)
        def _(n):
            cols = pl.ds(pl.multiple_of(n * TILE, TILE), TILE)
            x0, x1 = x_of(rx_f, chunk)
            pre = dot(x0, wg[0:HALF, cols]) + dot(x1, wg[HALF:D, cols])
            up = dot(x0, wu[0:HALF, cols]) + dot(x1, wu[HALF:D, cols])
            hid_a[:, cols] = (pre * lax.logistic(pre) * up).astype(BF16)

    def out_bwd(half, into):
        @pl.loop(0, HALF // TILE)
        def _(j):
            at = pl.ds(pl.multiple_of(half * HALF + j * TILE, TILE), TILE)
            got = dot(hid_a[...], wg[at, :], NT) + dot(hid_b[...], wu[at, :], NT)
            into[:, pl.ds(pl.multiple_of(j * TILE, TILE), TILE)] = got.astype(into.dtype)

    def out_fwd(half, into):
        @pl.loop(0, HALF // TILE)
        def _(j):
            at = pl.ds(pl.multiple_of(half * HALF + j * TILE, TILE), TILE)
            got = dot(hid_a[...], wd[:, at])
            into[:, pl.ds(pl.multiple_of(j * TILE, TILE), TILE)] = got.astype(into.dtype)

    class Return:
        def __init__(self, hidden, out, psend, precv, own, far, pr, home, ret, pick, tok, which, result):
            self.hidden, self.out = hidden, out
            self.psend, self.precv, self.own = psend, precv, own
            self.far, self.pr, self.home, self.ret = far, pr, home, ret
            self.pick, self.tok, self.which, self.result = pick, tok, which, result
            self.part, self.over, self.back = {}, {}, {}

        def give(self, chunk):
            self.out(1 - c, self.psend.at[chunk])
            self.part[chunk] = copy(self.psend.at[chunk], self.precv.at[chunk], other)
            self.part[chunk].start()

        def keep(self, chunk):
            self.out(c, self.own.at[chunk])

        def send_far(self):
            self.part[1].wait_recv()
            for k in (3, 2, 1, 0):
                self.far[rows(k)] = (
                    self.own[1, rows(k)] + self.precv[1, rows(k)].astype(F32)
                ).astype(BF16)
                self.over[k] = copy(self.far.at[rows(k)], self.pr.at[rows(k)], partner)
                self.over[k].start()

        def sum_near(self):
            self.part[0].wait_recv()

        def send_home(self, k):
            self.over[k].wait_recv()
            total = (
                self.own[0, rows(k)]
                + self.precv[0, rows(k)].astype(F32)
                + self.pr[rows(k)].astype(F32)
            ).astype(BF16)
            if k == 0:
                self.ret[rows(0)] = total
            else:
                self.home[rows(k)] = total
                self.back[k] = copy(self.home.at[rows(k)], self.ret.at[rows(k)], source[k])
                self.back[k].start()

        def finish(self):
            for k in (1, 2, 3):
                self.back[k].wait_recv()
            gate = meta[:, 256 + self.which * 128 : 384 + self.which * 128]
            gate = jnp.concatenate([gate, gate], axis=1)

            @pl.loop(0, HALF // TILE)
            def _(j):
                cols = pl.ds(pl.multiple_of(j * TILE, TILE), TILE)
                value = dot(self.pick[...], self.ret[:, cols])
                full = (self.tok[:, cols].astype(F32) + gate * value).astype(BF16)
                outs_send[self.which, :, cols] = full

            self.result[0, :, half_mine] = outs_send[self.which, mine, :]
            theirs = pl.ds(pl.multiple_of((1 - c) * TOK, TOK), TOK)
            self.last = copy(
                outs_send.at[self.which, theirs], outs_recv.at[self.which], other
            )
            self.last.start()

        def close(self):
            self.last.wait_recv()
            self.result[0, :, half_other] = outs_recv[self.which]

    rb = Return(
        hidden_bwd, out_bwd, b_psend, b_precv, b_own, b_far, b_pr, b_home, b_ret, b_pick, tok_g, 1, b_out
    )
    rf = Return(
        hidden_fwd, out_fwd, f_psend, f_precv, f_own, f_far, f_pr, f_home, f_ret, f_pick, tok_f, 0, f_out
    )

    own_saved.wait()
    swap_saved.wait_recv()
    ds.send()
    wait_g()
    dg.send()
    for k in (1, 2, 3):
        ds.relay(k)
    for k in (1, 2, 3):
        dg.relay(k)
    wait_f()
    df.send()
    for k in range(4):
        ds.hand(k)
    for k in range(4):
        dg.hand(k)
    for load in loads:
        load.wait()
    ds.ready(range(4, 8))
    dg.ready(range(4, 8))
    df.relay(1)
    rb.hidden(1)
    df.relay(2)
    rb.give(1)
    df.relay(3)
    rb.keep(1)
    rb.send_far()
    for k in range(4):
        df.hand(k)
    ds.ready(range(4))
    dg.ready(range(4))
    rb.hidden(0)
    rb.give(0)
    rb.keep(0)
    rb.sum_near()
    for k in (3, 2, 1, 0):
        rb.send_home(k)
    df.ready(range(4, 8))
    rf.hidden(1)
    rf.give(1)
    rf.keep(1)
    rf.send_far()
    df.ready(range(4))
    rf.hidden(0)
    rf.give(0)
    rf.keep(0)
    rf.sum_near()
    rb.finish()
    for k in (3, 2, 1, 0):
        rf.send_home(k)
    rb.close()
    rf.finish()
    rf.close()
    for cp in pending:
        cp.wait_send()


def local(*args):
    vmem = pl.BlockSpec(memory_space=pltpu.VMEM)
    hbm = pl.BlockSpec(memory_space=pl.ANY)
    tok = pltpu.VMEM((2 * TOK, HALF), BF16)
    block = pltpu.VMEM((ROWS, HALF), BF16)
    two = pltpu.VMEM((2, ROWS, HALF), BF16)
    held = pltpu.VMEM((2, 2 * ROWS, HALF), BF16)
    own = pltpu.VMEM((2, ROWS, HALF), F32)
    ret = pltpu.VMEM((256, HALF), BF16)
    stream = [two, two, own, block, block, block, ret]
    shape = jax.ShapeDtypeStruct((1, TOK, D), BF16)
    return pl.pallas_call(
        kernel,
        out_shape=(shape, shape),
        in_specs=[hbm, vmem, vmem, hbm, hbm, vmem, vmem, hbm, hbm, hbm],
        out_specs=(vmem, vmem),
        scratch_shapes=[
            pltpu.VMEM((D, HID), BF16),
            pltpu.VMEM((D, HID), BF16),
            pltpu.VMEM((HID, D), BF16),
            pltpu.VMEM((2 * TOK, 512), F32),
            pltpu.VMEM((256, 2 * TOK), BF16),
            pltpu.VMEM((256, 2 * TOK), BF16),
            pltpu.VMEM((2 * TOK, 256), BF16),
            pltpu.VMEM((2 * TOK, 256), BF16),
            tok,
            tok,
            tok,
            block,
            block,
            block,
            held,
            held,
            held,
            pltpu.VMEM((ROWS, HID), BF16),
            pltpu.VMEM((ROWS, HID), BF16),
            *stream,
            *stream,
            pltpu.VMEM((2, 2 * TOK, HALF), BF16),
            pltpu.VMEM((2, TOK, HALF), BF16),
            pltpu.SemaphoreType.DMA((N_SEM,)),
            pltpu.SemaphoreType.DMA((N_SEM,)),
            pltpu.SemaphoreType.DMA((4,)),
        ],
        compiler_params=pltpu.CompilerParams(
            collective_id=0, has_side_effects=True, vmem_limit_bytes=56 * 2**20
        ),
        cost_estimate=pl.CostEstimate(
            flops=16 * 2 * ROWS * D * HID, bytes_accessed=14 * 2**20, transcendentals=4 * ROWS * HID
        ),
    )(*args)


def solution(mesh):
    row = P("pipe", "expert", None)
    col = P("pipe", None, "expert")
    return jax.shard_map(
        local,
        mesh=mesh,
        in_specs=(row,) * 7 + (col, col, row),
        out_specs=(row, row),
        check_vma=False,
    )
```

```python
import functools

import jax
import jax.numpy as jnp
from jax import lax
from jax.experimental import pallas as pl
from jax.experimental.pallas import tpu as pltpu
from jax.sharding import PartitionSpec as P

D = 3584
HALF = D // 2
TOK = 64
HID = 512
MOST = 24
BLOCK = 2 * MOST
ROWS = 4 * BLOCK
TILE = 256
MESH = pl.DeviceIdType.MESH
F32 = jnp.float32
BF16 = jnp.bfloat16
NN = (((1,), (0,)), ((), ()))
NT = (((1,), (1,)), ((), ()))

N_SEM = 128


def dot(a, b, how=NN):
    return lax.dot_general(a, b, how, preferred_element_type=F32)


def kernel(
    acts,
    f_route,
    f_gate,
    saved,
    grads,
    b_route,
    b_gate,
    w_gate,
    w_up,
    w_down,
    f_out,
    b_out,
    wg,
    wu,
    wd,
    meta,
    gates,
    f_place,
    b_place,
    f_pick,
    b_pick,
    tok_s,
    tok_g,
    tok_f,
    pk_s,
    pk_g,
    pk_f,
    rx_s,
    rx_g,
    rx_f,
    hid_a,
    hid_b,
    b_psend,
    b_precv,
    b_own,
    b_far,
    b_pr,
    b_home,
    b_ret,
    f_psend,
    f_precv,
    f_own,
    f_far,
    f_pr,
    f_home,
    f_ret,
    outs_send,
    send_sem,
    recv_sem,
    load_sem,
):
    sec = lax.axis_index("pipe")
    ex = lax.axis_index("expert")
    n_sec = lax.axis_size("pipe")
    n_ex = lax.axis_size("expert")
    z = lax.div(ex, 2)
    c = lax.rem(ex, 2)
    sgn = 1 - 2 * lax.rem(z, 2)
    pair = lax.div(z, 2)

    def along(dist):
        return (sec, lax.rem(ex + 2 * dist * sgn + 2 * n_ex, n_ex))

    other = (sec, ex + 1 - 2 * c)
    partner = along(1)
    target = {1: along(-1), 2: along(2), 3: along(-3)}
    source = {1: along(-1), 2: along(-2), 3: along(-3)}
    nxt = lax.rem(sec + 1, n_sec)
    prv = lax.rem(sec + n_sec - 1, n_sec)

    count = [0]
    pending = []

    def copy(src, dst, to, sem=None):
        i = count[0]
        count[0] += 1
        out = pltpu.make_async_remote_copy(
            src_ref=src,
            dst_ref=dst,
            send_sem=send_sem.at[i],
            recv_sem=recv_sem.at[i] if sem is None else recv_sem.at[sem],
            device_id=to,
            device_id_type=MESH,
        )
        pending.append(out)
        return out

    loads = [
        pltpu.make_async_copy(w_gate.at[0], wg, load_sem.at[0]),
        pltpu.make_async_copy(w_up.at[0], wu, load_sem.at[1]),
        pltpu.make_async_copy(w_down.at[0], wd, load_sem.at[2]),
    ]
    mine = pl.ds(pl.multiple_of(c * TOK, TOK), TOK)
    half_mine = pl.ds(pl.multiple_of(c * HALF, HALF), HALF)
    half_other = pl.ds(pl.multiple_of((1 - c) * HALF, HALF), HALF)
    own_saved = pltpu.make_async_copy(
        saved.at[0, :, half_mine], tok_s.at[mine], load_sem.at[3]
    )
    own_saved.start()

    barrier = pltpu.get_barrier_semaphore()
    friends = [
        other,
        partner,
        along(-1),
        along(2),
        along(-2),
        along(-3),
        (nxt, 2 * z),
        (nxt, 2 * z + 1),
        (prv, 2 * z),
        (prv, 2 * z + 1),
    ]
    for friend in friends:
        pl.semaphore_signal(barrier, inc=1, device_id=friend, device_id_type=MESH)
    for load in loads:
        load.start()

    near_of = lax.broadcasted_iota(jnp.int32, (8, TOK), 0)
    row = lax.broadcasted_iota(jnp.int32, (TOK, TOK), 0)
    col = lax.broadcasted_iota(jnp.int32, (TOK, TOK), 1)
    above = jnp.where(row < col, 1.0, 0.0).astype(BF16)
    lines = []
    for route in (f_route, b_route):
        named = jnp.broadcast_to(route[...], (8, TOK))
        turn = lax.rem((named - pair) * sgn + 8, 4)
        near = jnp.where(turn == 0, 0, jnp.where(turn == 1, 2, jnp.where(turn == 2, 3, 1)))
        hot = jnp.where(near == near_of, 1.0, 0.0)
        before = dot(hot.astype(BF16), above)
        rank = jnp.sum(hot * before, axis=0, keepdims=True)
        lines.append((near[0:1] * BLOCK + c * MOST).astype(F32) + rank)
    lines += [f_gate[...], b_gate[...]]
    for at, line in enumerate(lines):
        meta[c, at : at + 1, :] = jnp.concatenate([line, line], axis=1)
    f_ret[ROWS:, :] = jnp.zeros((256 - ROWS, HALF), BF16)
    b_ret[ROWS:, :] = jnp.zeros((256 - ROWS, HALF), BF16)

    pl.semaphore_wait(barrier, len(friends))

    swap_meta = copy(meta.at[c], meta.at[c], other)
    swap_meta.start()
    swap_saved = copy(saved.at[0, :, half_other], tok_s.at[mine], other)
    swap_saved.start()

    def relay_pipe(tokens, land, to_sec):
        base = count[0]
        for half in range(2):
            cp = copy(
                tokens.at[0, :, half * HALF : half * HALF + HALF],
                land.at[mine],
                (to_sec, 2 * z + half),
                sem=base + c,
            )
            cp.start()

        def wait():
            for src in range(2):
                pltpu.make_async_remote_copy(
                    src_ref=tokens.at[0, :, 0:HALF],
                    dst_ref=land.at[src * TOK : src * TOK + TOK],
                    send_sem=send_sem.at[base],
                    recv_sem=recv_sem.at[base + src],
                    device_id=other,
                    device_id_type=MESH,
                ).wait_recv()

        return wait

    wait_g = relay_pipe(grads, tok_g, prv)
    wait_f = relay_pipe(acts, tok_f, nxt)

    def line_of(at):
        left = lax.broadcasted_iota(jnp.int32, (1, 2 * TOK), 1) < TOK
        return jnp.where(left, meta[0, at : at + 1, :], meta[1, at : at + 1, :])

    def make_place(which, place):
        slots = lax.broadcasted_iota(jnp.int32, (256, 2 * TOK), 0).astype(F32)
        hot = jnp.where(line_of(which) == slots, 1.0, 0.0)
        place[...] = hot.astype(BF16)

    def make_pick(which, pick):
        slots = lax.broadcasted_iota(jnp.int32, (256, 2 * TOK), 0).astype(F32)
        pick[...] = jnp.where(line_of(which) == slots, 1.0, 0.0).T.astype(BF16)

    def make_gate(which):
        gates[which] = jnp.broadcast_to(line_of(2 + which), (2 * TOK, 2 * TOK)).T

    def rows(k, n=1):
        return slice(k * BLOCK, (k + n) * BLOCK)

    class Dispatch:
        def __init__(self, tok, place, pk, rx):
            self.tok, self.place, self.pk, self.rx = tok, place, pk, rx
            self.near, self.over, self.cross = {}, {}, {}

        def send(self):
            for j in range(0, HALF, TILE):
                self.pk[:, j : j + TILE] = dot(
                    self.place[0:ROWS, :], self.tok[:, j : j + TILE]
                ).astype(BF16)
            self.rx[c, rows(0)] = self.pk[rows(0)]
            self.relay(0)
            for k in (1, 2):
                self.send_near(k)

        def send_near(self, k):
            self.near[k] = copy(self.pk.at[rows(k)], self.rx.at[c, rows(k)], target[k])
            self.near[k].start()

        def relay(self, k):
            if k:
                self.near[k].wait_recv()
            here = self.rx.at[c, rows(k)]
            self.over[k] = copy(here, self.rx.at[c, rows(4 + k)], partner)
            self.over[k].start()
            self.cross[k] = copy(here, here, other)
            self.cross[k].start()

        def hand(self, k):
            self.over[k].wait_recv()
            here = self.rx.at[c, rows(4 + k)]
            self.cross[4 + k] = copy(here, here, other)
            self.cross[4 + k].start()

        def ready(self, ks):
            for k in ks:
                self.cross[k].wait_recv()

    ds = Dispatch(tok_s, b_place, pk_s, rx_s)
    dg = Dispatch(tok_g, b_place, pk_g, rx_g)
    df = Dispatch(tok_f, f_place, pk_f, rx_f)

    def x_of(ref, chunk):
        first = chunk * ROWS
        return ref[0, first : first + ROWS, :], ref[1, first : first + ROWS, :]

    def hidden_bwd(chunk):
        @pl.loop(0, HID // TILE)
        def _(n):
            cols = pl.ds(pl.multiple_of(n * TILE, TILE), TILE)
            x0, x1 = x_of(rx_s, chunk)
            pre = dot(x0, wg[0:HALF, cols]) + dot(x1, wg[HALF:D, cols])
            up = dot(x0, wu[0:HALF, cols]) + dot(x1, wu[HALF:D, cols])
            g0, g1 = x_of(rx_g, chunk)
            back = dot(g0, wd[cols, 0:HALF], NT) + dot(g1, wd[cols, HALF:D], NT)
            sig = lax.logistic(pre)
            hid_b[:, cols] = (back * pre * sig).astype(BF16)
            hid_a[:, cols] = (back * up * sig * (1.0 + pre * (1.0 - sig))).astype(BF16)

    def hidden_fwd(chunk):
        @pl.loop(0, HID // TILE)
        def _(n):
            cols = pl.ds(pl.multiple_of(n * TILE, TILE), TILE)
            x0, x1 = x_of(rx_f, chunk)
            pre = dot(x0, wg[0:HALF, cols]) + dot(x1, wg[HALF:D, cols])
            up = dot(x0, wu[0:HALF, cols]) + dot(x1, wu[HALF:D, cols])
            hid_a[:, cols] = (pre * lax.logistic(pre) * up).astype(BF16)

    def out_bwd(half, into):
        @pl.loop(0, HALF // TILE)
        def _(j):
            at = pl.ds(pl.multiple_of(half * HALF + j * TILE, TILE), TILE)
            got = dot(hid_a[...], wg[at, :], NT) + dot(hid_b[...], wu[at, :], NT)
            into[:, pl.ds(pl.multiple_of(j * TILE, TILE), TILE)] = got.astype(into.dtype)

    def out_fwd(half, into):
        @pl.loop(0, HALF // TILE)
        def _(j):
            at = pl.ds(pl.multiple_of(half * HALF + j * TILE, TILE), TILE)
            got = dot(hid_a[...], wd[:, at])
            into[:, pl.ds(pl.multiple_of(j * TILE, TILE), TILE)] = got.astype(into.dtype)

    class Return:
        def __init__(self, hidden, out, psend, precv, own, far, pr, home, ret, pick, tok, which, result):
            self.hidden, self.out = hidden, out
            self.psend, self.precv, self.own = psend, precv, own
            self.far, self.pr, self.home, self.ret = far, pr, home, ret
            self.pick, self.tok, self.which, self.result = pick, tok, which, result
            self.part, self.over, self.back = {}, {}, {}

        def give(self, chunk):
            self.out(1 - c, self.psend.at[chunk])
            self.part[chunk] = copy(self.psend.at[chunk], self.precv.at[chunk], other)
            self.part[chunk].start()

        def keep(self, chunk):
            self.out(c, self.own.at[chunk])

        def send_far(self):
            self.part[1].wait_recv()
            for k in (3, 2, 1, 0):
                self.far[rows(k)] = (
                    self.own[1, rows(k)] + self.precv[1, rows(k)].astype(F32)
                ).astype(BF16)
                self.over[k] = copy(self.far.at[rows(k)], self.pr.at[rows(k)], partner)
                self.over[k].start()

        def sum_near(self):
            self.part[0].wait_recv()

        def send_home(self, k):
            self.over[k].wait_recv()
            total = (
                self.own[0, rows(k)]
                + self.precv[0, rows(k)].astype(F32)
                + self.pr[rows(k)].astype(F32)
            ).astype(BF16)
            if k == 0:
                self.ret[rows(0)] = total
            else:
                self.home[rows(k)] = total
                self.back[k] = copy(self.home.at[rows(k)], self.ret.at[rows(k)], source[k])
                self.back[k].start()

        def finish(self):
            for k in (1, 2, 3):
                self.back[k].wait_recv()
            gate = gates[self.which]
            gate = jnp.concatenate([gate, gate], axis=1)
            theirs = pl.ds(pl.multiple_of((1 - c) * TOK, TOK), TOK)
            self.last = []
            for first, last in ((0, 4), (4, 7)):

                @pl.loop(first, last)
                def _(j):
                    cols = pl.ds(pl.multiple_of(j * TILE, TILE), TILE)
                    value = dot(self.pick[...], self.ret[:, cols])
                    full = (self.tok[:, cols].astype(F32) + gate * value).astype(BF16)
                    outs_send[self.which, :, cols] = full

                span = slice(first * TILE, last * TILE)
                land = pl.ds(pl.multiple_of(c * HALF + first * TILE, TILE), (last - first) * TILE)
                part = copy(
                    outs_send.at[self.which, theirs, span], self.result.at[0, :, land], other
                )
                part.start()
                self.last.append(part)
                self.result[0, :, land] = outs_send[self.which, mine, span]

        def close(self):
            for part in self.last:
                part.wait_recv()

    rb = Return(
        hidden_bwd, out_bwd, b_psend, b_precv, b_own, b_far, b_pr, b_home, b_ret, b_pick, tok_g, 1, b_out
    )
    rf = Return(
        hidden_fwd, out_fwd, f_psend, f_precv, f_own, f_far, f_pr, f_home, f_ret, f_pick, tok_f, 0, f_out
    )

    swap_meta.wait_recv()
    make_place(1, b_place)
    own_saved.wait()
    swap_saved.wait_recv()
    ds.send()
    make_place(0, f_place)
    make_pick(0, f_pick)
    make_pick(1, b_pick)
    make_gate(0)
    make_gate(1)
    ds.relay(1)
    ds.send_near(3)
    wait_g()
    dg.send()
    dg.send_near(3)
    ds.relay(2)
    ds.relay(3)
    dg.relay(1)
    wait_f()
    df.send()
    df.send_near(3)
    dg.relay(2)
    dg.relay(3)
    for k in range(4):
        ds.hand(k)
    df.relay(1)
    dg.hand(0)
    df.relay(2)
    dg.hand(1)
    df.relay(3)
    dg.hand(2)
    dg.hand(3)
    for load in loads:
        load.wait()
    ds.ready(range(4, 8))
    dg.ready(range(4, 8))
    rb.hidden(1)
    rb.give(1)
    rb.keep(1)
    rb.send_far()
    ds.ready(range(4))
    dg.ready(range(4))
    rb.hidden(0)
    for k in range(4):
        df.hand(k)
    rb.give(0)
    rb.keep(0)
    rb.sum_near()
    df.ready(range(4, 8))
    rf.hidden(1)
    rb.send_home(3)
    rf.give(1)
    rb.send_home(2)
    rf.keep(1)
    rb.send_home(1)
    rf.send_far()
    rb.send_home(0)
    df.ready(range(4))
    rf.hidden(0)
    rf.give(0)
    rf.keep(0)
    rf.sum_near()
    for k in (3, 2, 1):
        rf.send_home(k)
    rb.finish()
    rf.send_home(0)
    rb.close()
    rf.finish()
    rf.close()
    for cp in pending:
        cp.wait_send()


def local(acts, f_route, f_gate, saved, grads, b_route, b_gate, w_gate, w_up, w_down):
    small = [v.reshape(1, TOK) for v in (f_route, f_gate, b_route, b_gate)]
    args = (acts, *small[:2], saved, grads, *small[2:], w_gate, w_up, w_down)
    vmem = pl.BlockSpec(memory_space=pltpu.VMEM)
    hbm = pl.BlockSpec(memory_space=pl.ANY)
    tok = pltpu.VMEM((2 * TOK, HALF), BF16)
    block = pltpu.VMEM((ROWS, HALF), BF16)
    two = pltpu.VMEM((2, ROWS, HALF), BF16)
    held = pltpu.VMEM((2, 2 * ROWS, HALF), BF16)
    own = pltpu.VMEM((2, ROWS, HALF), F32)
    ret = pltpu.VMEM((256, HALF), BF16)
    stream = [two, two, own, block, block, block, ret]
    shape = jax.ShapeDtypeStruct((1, TOK, D), BF16)
    return pl.pallas_call(
        kernel,
        out_shape=(pltpu.VMEM((1, TOK, D), BF16),) * 2,
        in_specs=[hbm, vmem, vmem, hbm, hbm, vmem, vmem, hbm, hbm, hbm],
        out_specs=(vmem, vmem),
        scratch_shapes=[
            pltpu.VMEM((D, HID), BF16),
            pltpu.VMEM((D, HID), BF16),
            pltpu.VMEM((HID, D), BF16),
            pltpu.VMEM((2, 8, 2 * TOK), F32),
            pltpu.VMEM((2, 2 * TOK, 2 * TOK), F32),
            pltpu.VMEM((256, 2 * TOK), BF16),
            pltpu.VMEM((256, 2 * TOK), BF16),
            pltpu.VMEM((2 * TOK, 256), BF16),
            pltpu.VMEM((2 * TOK, 256), BF16),
            tok,
            tok,
            tok,
            block,
            block,
            block,
            held,
            held,
            held,
            pltpu.VMEM((ROWS, HID), BF16),
            pltpu.VMEM((ROWS, HID), BF16),
            *stream,
            *stream,
            pltpu.VMEM((2, 2 * TOK, HALF), BF16),
            pltpu.SemaphoreType.DMA((N_SEM,)),
            pltpu.SemaphoreType.DMA((N_SEM,)),
            pltpu.SemaphoreType.DMA((4,)),
        ],
        compiler_params=pltpu.CompilerParams(
            collective_id=0, has_side_effects=True, vmem_limit_bytes=56 * 2**20
        ),
        cost_estimate=pl.CostEstimate(
            flops=16 * 2 * ROWS * D * HID, bytes_accessed=14 * 2**20, transcendentals=4 * ROWS * HID
        ),
    )(*args)


def solution(mesh):
    row = P("pipe", "expert", None)
    col = P("pipe", None, "expert")
    return jax.shard_map(
        local,
        mesh=mesh,
        in_specs=(row,) * 7 + (col, col, row),
        out_specs=(row, row),
        check_vma=False,
    )
```

```python
import functools

import jax
import jax.numpy as jnp
from jax import lax
from jax.experimental import pallas as pl
from jax.experimental.pallas import tpu as pltpu
from jax.sharding import PartitionSpec as P

D = 3584
HALF = D // 2
TOK = 64
HID = 512
MOST = 24
BLOCK = 2 * MOST
ROWS = 4 * BLOCK
TILE = 256
MESH = pl.DeviceIdType.MESH
F32 = jnp.float32
BF16 = jnp.bfloat16
NN = (((1,), (0,)), ((), ()))
NT = (((1,), (1,)), ((), ()))

N_SEM = 128
WHOLE = (slice(0, HALF),)
PARTS = (slice(0, 4 * TILE), slice(4 * TILE, HALF))


def dot(a, b, how=NN):
    return lax.dot_general(a, b, how, preferred_element_type=F32)


def kernel(
    acts,
    f_route,
    f_gate,
    saved,
    grads,
    b_route,
    b_gate,
    w_gate,
    w_up,
    w_down,
    f_out,
    b_out,
    wg,
    wu,
    wd,
    routes,
    weights,
    notes,
    gates,
    f_place,
    b_place,
    f_pick,
    b_pick,
    tok_s,
    tok_g,
    tok_f,
    pk_s,
    pk_g,
    pk_f,
    rx_s,
    rx_g,
    rx_f,
    hid_a,
    hid_b,
    b_psend,
    b_precv,
    b_own,
    b_far,
    b_pr,
    b_home,
    b_ret,
    f_psend,
    f_precv,
    f_own,
    f_far,
    f_pr,
    f_home,
    f_ret,
    outs_send,
    send_sem,
    recv_sem,
    load_sem,
):
    sec = lax.axis_index("pipe")
    ex = lax.axis_index("expert")
    n_sec = lax.axis_size("pipe")
    n_ex = lax.axis_size("expert")
    z = lax.div(ex, 2)
    c = lax.rem(ex, 2)
    sgn = 1 - 2 * lax.rem(z, 2)
    pair = lax.div(z, 2)

    def along(dist):
        return (sec, lax.rem(ex + 2 * dist * sgn + 2 * n_ex, n_ex))

    other = (sec, ex + 1 - 2 * c)
    partner = along(1)
    target = {1: along(-1), 2: along(2), 3: along(-3)}
    source = {1: along(-1), 2: along(-2), 3: along(-3)}
    nxt = lax.rem(sec + 1, n_sec)
    prv = lax.rem(sec + n_sec - 1, n_sec)

    def order_at(chip):
        second, eighth = jnp.where(chip == 2, 1, 0), jnp.where(chip == 7, 1, 0)
        return 3 - second - 2 * eighth, 2 - second, 1 + 2 * (second + eighth)

    count = [0]
    pending = []

    def copy(src, dst, to, sem=None):
        i = count[0]
        count[0] += 1
        out = pltpu.make_async_remote_copy(
            src_ref=src,
            dst_ref=dst,
            send_sem=send_sem.at[i],
            recv_sem=recv_sem.at[i] if sem is None else recv_sem.at[sem],
            device_id=to,
            device_id_type=MESH,
        )
        pending.append(out)
        return out

    loads = [
        pltpu.make_async_copy(w_gate.at[0], wg, load_sem.at[0]),
        pltpu.make_async_copy(w_up.at[0], wu, load_sem.at[1]),
        pltpu.make_async_copy(w_down.at[0], wd, load_sem.at[2]),
    ]
    mine = pl.ds(pl.multiple_of(c * TOK, TOK), TOK)
    half_mine = pl.ds(pl.multiple_of(c * HALF, HALF), HALF)
    half_other = pl.ds(pl.multiple_of((1 - c) * HALF, HALF), HALF)
    own_saved = pltpu.make_async_copy(
        saved.at[0, :, half_mine], tok_s.at[mine], load_sem.at[3]
    )
    small = ((routes, (f_route, b_route)), (weights, (f_gate, b_gate)))
    small_loads = []
    for which in (1, 0):
        for kind, (held, given) in enumerate(small):
            at = load_sem.at[4 + 2 * which + kind]
            small_loads.append(pltpu.make_async_copy(given[which], held.at[which], at))

    barrier = pltpu.get_barrier_semaphore()
    friends = [
        other,
        partner,
        along(-1),
        along(2),
        along(-2),
        along(-3),
        (nxt, 2 * z),
        (nxt, 2 * z + 1),
        (prv, 2 * z),
        (prv, 2 * z + 1),
    ]
    for friend in friends:
        pl.semaphore_signal(barrier, inc=1, device_id=friend, device_id_type=MESH)
    for load in (*small_loads, own_saved, *loads):
        load.start()

    pl.semaphore_wait(barrier, len(friends))

    swap_saved = copy(saved.at[0, :, half_other], tok_s.at[mine], other)
    swap_saved.start()
    for load in small_loads:
        load.wait()
    for which in range(2):
        notes[c, which : which + 1, 0:TOK] = routes[which].astype(F32)
        notes[c, 2 + which : 3 + which, 0:TOK] = weights[which]
    swap_notes = copy(notes.at[c], notes.at[c], other)
    swap_notes.start()

    def relay_pipe(tokens, land, to_sec):
        base = count[0]
        for half in range(2):
            cp = copy(
                tokens.at[0, :, half * HALF : half * HALF + HALF],
                land.at[mine],
                (to_sec, 2 * z + half),
                sem=base + c,
            )
            cp.start()

        def wait():
            for src in range(2):
                pltpu.make_async_remote_copy(
                    src_ref=tokens.at[0, :, 0:HALF],
                    dst_ref=land.at[src * TOK : src * TOK + TOK],
                    send_sem=send_sem.at[base],
                    recv_sem=recv_sem.at[base + src],
                    device_id=other,
                    device_id_type=MESH,
                ).wait_recv()

        return wait

    wait_g = relay_pipe(grads, tok_g, prv)
    wait_f = relay_pipe(acts, tok_f, nxt)

    def both(at):
        return jnp.concatenate([notes[0, at : at + 1, 0:TOK], notes[1, at : at + 1, 0:TOK]], axis=1)

    def slots_of(which):
        tokens = 2 * TOK
        named = jnp.broadcast_to(both(which).astype(jnp.int32), (8, tokens))
        turn = jnp.bitwise_and((named - pair) * sgn + 8, 3)
        near = jnp.where(turn == 0, 0, jnp.where(turn == 1, 2, jnp.where(turn == 2, 3, 1)))
        hot = jnp.where(near == lax.broadcasted_iota(jnp.int32, (8, tokens), 0), 1.0, 0.0)
        row = lax.broadcasted_iota(jnp.int32, (tokens, tokens), 0)
        col = lax.broadcasted_iota(jnp.int32, (tokens, tokens), 1)
        ahead = (row < col) & ((row < TOK) == (col < TOK))
        before = dot(hot.astype(BF16), jnp.where(ahead, 1.0, 0.0).astype(BF16))
        rank = jnp.sum(hot * before, axis=0, keepdims=True)
        core = jnp.where(lax.broadcasted_iota(jnp.int32, (1, tokens), 1) < TOK, 0, MOST)
        return (near[0:1] * BLOCK + core).astype(F32) + rank

    def hot_of(line):
        slots = lax.broadcasted_iota(jnp.int32, (256, 2 * TOK), 0).astype(F32)
        return jnp.where(line == slots, 1.0, 0.0)

    def make_gate(which):
        line = jnp.broadcast_to(both(2 + which), (2 * TOK, 2 * TOK))
        gates[which] = line.T

    def rows(k, n=1):
        return slice(k * BLOCK, (k + n) * BLOCK)

    def span_of(k):
        if isinstance(k, int):
            return rows(k)
        return pl.ds(pl.multiple_of(k * BLOCK, BLOCK), BLOCK)

    def arrival(src, dst, sem):
        pltpu.make_async_remote_copy(
            src_ref=src,
            dst_ref=dst,
            send_sem=send_sem.at[0],
            recv_sem=recv_sem.at[sem],
            device_id=other,
            device_id_type=MESH,
        ).wait_recv()

    class Dispatch:
        def __init__(self, tok, place, pk, rx):
            self.tok, self.place, self.pk, self.rx = tok, place, pk, rx
            self.near, self.over, self.cross = {}, {}, {}

        def send(self):
            for j in range(0, HALF, TILE):
                self.pk[:, j : j + TILE] = dot(
                    self.place[0:ROWS, :], self.tok[:, j : j + TILE]
                ).astype(BF16)
            self.rx[c, rows(0)] = self.pk[rows(0)]
            self.relay(0)
            for k in (1, 2):
                self.send_near(k)

        def send_near(self, k):
            self.near[k] = copy(self.pk.at[rows(k)], self.rx.at[c, rows(k)], target[k])
            self.near[k].start()

        def relay(self, k):
            if k:
                self.near[k].wait_recv()
            here = self.rx.at[c, rows(k)]
            self.over[k] = copy(here, self.rx.at[c, rows(4 + k)], partner)
            self.over[k].start()
            self.cross[k] = copy(here, here, other)
            self.cross[k].start()

        def hand(self, k):
            self.over[k].wait_recv()
            here = self.rx.at[c, rows(4 + k)]
            self.cross[4 + k] = copy(here, here, other)
            self.cross[4 + k].start()

        def ready(self, ks):
            for k in ks:
                self.cross[k].wait_recv()

    ds = Dispatch(tok_s, b_place, pk_s, rx_s)
    dg = Dispatch(tok_g, b_place, pk_g, rx_g)
    df = Dispatch(tok_f, f_place, pk_f, rx_f)

    def x_of(ref, chunk):
        first = chunk * ROWS
        return ref[0, first : first + ROWS, :], ref[1, first : first + ROWS, :]

    def hidden_bwd(chunk):
        @pl.loop(0, HID // TILE)
        def _(n):
            cols = pl.ds(pl.multiple_of(n * TILE, TILE), TILE)
            x0, x1 = x_of(rx_s, chunk)
            pre = dot(x0, wg[0:HALF, cols]) + dot(x1, wg[HALF:D, cols])
            up = dot(x0, wu[0:HALF, cols]) + dot(x1, wu[HALF:D, cols])
            g0, g1 = x_of(rx_g, chunk)
            back = dot(g0, wd[cols, 0:HALF], NT) + dot(g1, wd[cols, HALF:D], NT)
            sig = lax.logistic(pre)
            hid_b[:, cols] = (back * pre * sig).astype(BF16)
            hid_a[:, cols] = (back * up * sig * (1.0 + pre * (1.0 - sig))).astype(BF16)

    def hidden_fwd(chunk):
        @pl.loop(0, HID // TILE)
        def _(n):
            cols = pl.ds(pl.multiple_of(n * TILE, TILE), TILE)
            x0, x1 = x_of(rx_f, chunk)
            pre = dot(x0, wg[0:HALF, cols]) + dot(x1, wg[HALF:D, cols])
            up = dot(x0, wu[0:HALF, cols]) + dot(x1, wu[HALF:D, cols])
            hid_a[:, cols] = (pre * lax.logistic(pre) * up).astype(BF16)

    def out_bwd(half, into):
        @pl.loop(0, HALF // TILE)
        def _(j):
            at = pl.ds(pl.multiple_of(half * HALF + j * TILE, TILE), TILE)
            got = dot(hid_a[...], wg[at, :], NT) + dot(hid_b[...], wu[at, :], NT)
            into[:, pl.ds(pl.multiple_of(j * TILE, TILE), TILE)] = got.astype(into.dtype)

    def out_fwd(half, into):
        @pl.loop(0, HALF // TILE)
        def _(j):
            at = pl.ds(pl.multiple_of(half * HALF + j * TILE, TILE), TILE)
            got = dot(hid_a[...], wd[:, at])
            into[:, pl.ds(pl.multiple_of(j * TILE, TILE), TILE)] = got.astype(into.dtype)

    class Return:
        def __init__(self, hidden, out, psend, precv, own, far, pr, home, ret, pick, tok, which, result, spans, far_order):
            self.hidden, self.out = hidden, out
            self.psend, self.precv, self.own = psend, precv, own
            self.far, self.pr, self.home, self.ret = far, pr, home, ret
            self.pick, self.tok, self.which, self.result = pick, tok, which, result
            self.part, self.over, self.back, self.last = {}, {}, {}, []
            self.spans, self.far_order = spans, far_order

        def give(self, chunk):
            self.out(1 - c, self.psend.at[chunk])
            self.part[chunk] = copy(self.psend.at[chunk], self.precv.at[chunk], other)
            self.part[chunk].start()

        def keep(self, chunk):
            self.out(c, self.own.at[chunk])

        def send_far(self):
            self.part[1].wait_recv()
            for n, cols in enumerate(self.spans):
                base = count[0]
                for k in (*self.far_order, 0):
                    at = span_of(k)
                    self.far[at, cols] = (
                        self.own[1, at, cols] + self.precv[1, at, cols].astype(F32)
                    ).astype(BF16)
                    copy(self.far.at[at, cols], self.pr.at[at, cols], partner, sem=base + k).start()
                self.over[n] = base

        def sum_near(self):
            self.part[0].wait_recv()

        def send_home(self, k, n=0):
            cols = self.spans[n]
            at = span_of(k)
            arrival(self.far.at[at, cols], self.pr.at[at, cols], self.over[n] + k)
            total = (
                self.own[0, at, cols]
                + self.precv[0, at, cols].astype(F32)
                + self.pr[at, cols].astype(F32)
            ).astype(BF16)
            if isinstance(k, int) and k == 0:
                self.ret[at, cols] = total
            else:
                self.home[at, cols] = total
                if n not in self.back:
                    self.back[n] = count[0]
                    count[0] += 3
                copy(
                    self.home.at[at, cols],
                    self.ret.at[at, cols],
                    along(-k),
                    sem=self.back[n] + k - 1,
                ).start()

        def finish(self, n=0):
            for k in (1, 2, 3):
                at = span_of(k)
                arrival(self.home.at[at, self.spans[n]], self.ret.at[at, self.spans[n]], self.back[n] + k - 1)
            gate = gates[self.which]
            gate = jnp.concatenate([gate, gate], axis=1)
            theirs = pl.ds(pl.multiple_of((1 - c) * TOK, TOK), TOK)
            span = self.spans[n]
            width = span.stop - span.start

            @pl.loop(span.start // TILE, span.stop // TILE)
            def _(j):
                cols = pl.ds(pl.multiple_of(j * TILE, TILE), TILE)
                value = dot(self.pick[...], self.ret[:, cols])
                full = (self.tok[:, cols].astype(F32) + gate * value).astype(BF16)
                outs_send[self.which, :, cols] = full

            land = pl.ds(pl.multiple_of(c * HALF + span.start, TILE), width)
            part = copy(outs_send.at[self.which, theirs, span], self.result.at[0, :, land], other)
            part.start()
            self.last.append(part)
            self.result[0, :, land] = outs_send[self.which, mine, span]

        def close(self):
            for part in self.last:
                part.wait_recv()

    rb = Return(
        hidden_bwd, out_bwd, b_psend, b_precv, b_own, b_far, b_pr, b_home, b_ret, b_pick, tok_g, 1, b_out, WHOLE, (3, 2, 1)
    )
    rf = Return(
        hidden_fwd, out_fwd, f_psend, f_precv, f_own, f_far, f_pr, f_home, f_ret, f_pick, tok_f, 0, f_out, WHOLE, order_at(z + sgn)
    )

    swap_notes.wait_recv()
    b_line = slots_of(1)
    b_place[...] = hot_of(b_line).astype(BF16)
    own_saved.wait()
    swap_saved.wait_recv()
    ds.send()
    f_line = slots_of(0)
    f_place[...] = hot_of(f_line).astype(BF16)
    b_pick[...] = hot_of(b_line).T.astype(BF16)
    f_pick[...] = hot_of(f_line).T.astype(BF16)
    make_gate(0)
    make_gate(1)
    f_ret[ROWS:, :] = jnp.zeros((256 - ROWS, HALF), BF16)
    b_ret[ROWS:, :] = jnp.zeros((256 - ROWS, HALF), BF16)
    ds.relay(1)
    ds.send_near(3)
    wait_g()
    dg.send()
    dg.send_near(3)
    ds.relay(2)
    ds.relay(3)
    dg.relay(1)
    wait_f()
    df.send()
    df.send_near(3)
    dg.relay(2)
    dg.relay(3)
    for k in range(4):
        ds.hand(k)
    df.relay(1)
    dg.hand(0)
    df.relay(2)
    dg.hand(1)
    df.relay(3)
    dg.hand(2)
    dg.hand(3)
    for load in loads:
        load.wait()
    ds.ready(range(4, 8))
    dg.ready(range(4, 8))
    rb.hidden(1)
    rb.give(1)
    rb.keep(1)
    rb.send_far()
    ds.ready(range(4))
    dg.ready(range(4))
    rb.hidden(0)
    for k in range(4):
        df.hand(k)
    rb.give(0)
    rb.keep(0)
    rb.sum_near()
    df.ready(range(4, 8))
    rf.hidden(1)
    rb.send_home(3)
    rf.give(1)
    rb.send_home(2)
    rf.keep(1)
    rb.send_home(1)
    rf.send_far()
    rb.send_home(0)
    df.ready(range(4))
    rf.hidden(0)
    rf.give(0)
    rf.keep(0)
    rf.sum_near()
    for k in order_at(z):
        rf.send_home(k)
    rb.finish()
    rf.send_home(0)
    rb.close()
    rf.finish()
    rf.close()
    for cp in pending:
        cp.wait_send()


def hand_on(f_in, b_in, f_res, b_res, sem):
    moves = [
        pltpu.make_async_copy(f_in, f_res, sem.at[0]),
        pltpu.make_async_copy(b_in, b_res, sem.at[1]),
    ]
    for move in moves:
        move.start()
    for move in moves:
        move.wait()


def local(acts, f_route, f_gate, saved, grads, b_route, b_gate, w_gate, w_up, w_down):
    small = [v.reshape(1, TOK) for v in (f_route, f_gate, b_route, b_gate)]
    args = (acts, *small[:2], saved, grads, *small[2:], w_gate, w_up, w_down)
    vmem = pl.BlockSpec(memory_space=pltpu.VMEM)
    hbm = pl.BlockSpec(memory_space=pl.ANY)
    tok = pltpu.VMEM((2 * TOK, HALF), BF16)
    block = pltpu.VMEM((ROWS, HALF), BF16)
    two = pltpu.VMEM((2, ROWS, HALF), BF16)
    held = pltpu.VMEM((2, 2 * ROWS, HALF), BF16)
    own = pltpu.VMEM((2, ROWS, HALF), F32)
    ret = pltpu.VMEM((256, HALF), BF16)
    stream = [two, two, own, block, block, block, ret]
    shape = jax.ShapeDtypeStruct((1, TOK, D), BF16)
    got = pl.pallas_call(
        kernel,
        out_shape=(pltpu.VMEM((1, TOK, D), BF16),) * 2,
        in_specs=[hbm] * 10,
        out_specs=(vmem, vmem),
        scratch_shapes=[
            pltpu.VMEM((D, HID), BF16),
            pltpu.VMEM((D, HID), BF16),
            pltpu.VMEM((HID, D), BF16),
            pltpu.VMEM((2, 1, TOK), jnp.int32),
            pltpu.VMEM((2, 1, TOK), F32),
            pltpu.VMEM((2, 8, 2 * TOK), F32),
            pltpu.VMEM((2, 2 * TOK, 2 * TOK), F32),
            pltpu.VMEM((256, 2 * TOK), BF16),
            pltpu.VMEM((256, 2 * TOK), BF16),
            pltpu.VMEM((2 * TOK, 256), BF16),
            pltpu.VMEM((2 * TOK, 256), BF16),
            tok,
            tok,
            tok,
            block,
            block,
            block,
            held,
            held,
            held,
            pltpu.VMEM((ROWS, HID), BF16),
            pltpu.VMEM((ROWS, HID), BF16),
            *stream,
            *stream,
            pltpu.VMEM((2, 2 * TOK, HALF), BF16),
            pltpu.SemaphoreType.DMA((N_SEM,)),
            pltpu.SemaphoreType.DMA((N_SEM,)),
            pltpu.SemaphoreType.DMA((8,)),
        ],
        compiler_params=pltpu.CompilerParams(
            collective_id=0, has_side_effects=True, vmem_limit_bytes=56 * 2**20
        ),
        cost_estimate=pl.CostEstimate(
            flops=16 * 2 * ROWS * D * HID, bytes_accessed=14 * 2**20, transcendentals=4 * ROWS * HID
        ),
    )(*args)
    return pl.pallas_call(
        hand_on,
        out_shape=(shape, shape),
        in_specs=[vmem, vmem],
        out_specs=(hbm, hbm),
        scratch_shapes=[pltpu.SemaphoreType.DMA((2,))],
    )(*(pltpu.with_memory_space_constraint(v, pltpu.VMEM) for v in got))


def solution(mesh):
    row = P("pipe", "expert", None)
    col = P("pipe", None, "expert")
    return jax.shard_map(
        local,
        mesh=mesh,
        in_specs=(row,) * 7 + (col, col, row),
        out_specs=(row, row),
        check_vma=False,
    )
```

```python
import functools

import jax
import jax.numpy as jnp
from jax import lax
from jax.experimental import pallas as pl
from jax.experimental.pallas import tpu as pltpu
from jax.sharding import PartitionSpec as P

D = 3584
HALF = D // 2
TOK = 64
HID = 512
MOST = 24
BLOCK = 2 * MOST
ROWS = 4 * BLOCK
TILE = 256
MESH = pl.DeviceIdType.MESH
F32 = jnp.float32
BF16 = jnp.bfloat16
NN = (((1,), (0,)), ((), ()))
NT = (((1,), (1,)), ((), ()))

N_SEM = 128
WHOLE = (slice(0, HALF),)
PARTS = (slice(0, 4 * TILE), slice(4 * TILE, HALF))


def dot(a, b, how=NN):
    return lax.dot_general(a, b, how, preferred_element_type=F32)


def kernel(
    acts,
    f_route,
    f_gate,
    saved,
    grads,
    b_route,
    b_gate,
    w_gate,
    w_up,
    w_down,
    f_out,
    b_out,
    wg,
    wu,
    wd,
    routes,
    weights,
    notes,
    gates,
    f_place,
    b_place,
    f_pick,
    b_pick,
    tok_s,
    tok_g,
    tok_f,
    pk_s,
    pk_g,
    pk_f,
    rx_s,
    rx_g,
    rx_f,
    hid_a,
    hid_b,
    b_psend,
    b_precv,
    b_own,
    b_far,
    b_pr,
    b_home,
    b_ret,
    f_psend,
    f_precv,
    f_own,
    f_far,
    f_pr,
    f_home,
    f_ret,
    outs_send,
    send_sem,
    recv_sem,
    load_sem,
    ready,
):
    sec = lax.axis_index("pipe")
    ex = lax.axis_index("expert")
    n_sec = lax.axis_size("pipe")
    n_ex = lax.axis_size("expert")
    z = lax.div(ex, 2)
    c = lax.rem(ex, 2)
    sgn = 1 - 2 * lax.rem(z, 2)
    pair = lax.div(z, 2)

    def along(dist):
        return (sec, lax.rem(ex + 2 * dist * sgn + 2 * n_ex, n_ex))

    other = (sec, ex + 1 - 2 * c)
    partner = along(1)
    target = {1: along(-1), 2: along(2), 3: along(-3)}
    source = {1: along(-1), 2: along(-2), 3: along(-3)}
    nxt = lax.rem(sec + 1, n_sec)
    prv = lax.rem(sec + n_sec - 1, n_sec)

    def order_at(chip):
        second, eighth = jnp.where(chip == 2, 1, 0), jnp.where(chip == 7, 1, 0)
        return 3 - second - 2 * eighth, 2 - second, 1 + 2 * (second + eighth)

    count = [0]
    pending = []

    def copy(src, dst, to, sem=None):
        i = count[0]
        count[0] += 1
        out = pltpu.make_async_remote_copy(
            src_ref=src,
            dst_ref=dst,
            send_sem=send_sem.at[i],
            recv_sem=recv_sem.at[i] if sem is None else recv_sem.at[sem],
            device_id=to,
            device_id_type=MESH,
        )
        pending.append(out)
        return out

    loads = [
        pltpu.make_async_copy(w_gate.at[0], wg, load_sem.at[0]),
        pltpu.make_async_copy(w_up.at[0], wu, load_sem.at[1]),
        pltpu.make_async_copy(w_down.at[0], wd, load_sem.at[2]),
    ]
    mine = pl.ds(pl.multiple_of(c * TOK, TOK), TOK)
    half_mine = pl.ds(pl.multiple_of(c * HALF, HALF), HALF)
    half_other = pl.ds(pl.multiple_of((1 - c) * HALF, HALF), HALF)
    own_saved = pltpu.make_async_copy(
        saved.at[0, :, half_mine], tok_s.at[mine], load_sem.at[3]
    )
    small = ((routes, (f_route, b_route)), (weights, (f_gate, b_gate)))
    small_loads = []
    for which in (1, 0):
        for kind, (held, given) in enumerate(small):
            at = load_sem.at[4 + 2 * which + kind]
            small_loads.append(pltpu.make_async_copy(given[which], held.at[which], at))

    barrier = pltpu.get_barrier_semaphore()
    for dist in (1, -1, 2, -2, -3):
        there = along(dist)
        pl.semaphore_signal(
            barrier, inc=1, device_id=(there[0], there[1] - c), device_id_type=MESH
        )

    @pl.when(c == 1)
    def _():
        pl.semaphore_signal(barrier, inc=1, device_id=other, device_id_type=MESH)

    for there in (nxt, prv):
        pl.semaphore_signal(barrier, inc=1, device_id=(there, 2 * z + 1), device_id_type=MESH)
    for load in (*small_loads, own_saved, *loads):
        load.start()

    @pl.when(c == 0)
    def _():
        pl.semaphore_wait(barrier, 11)
        pl.semaphore_signal(ready, inc=1, device_id=other, device_id_type=MESH)

    @pl.when(c == 1)
    def _():
        pl.semaphore_wait(ready, 1)

    def sections_ready():
        @pl.when(c == 1)
        def _():
            pl.semaphore_wait(barrier, 4)
            pl.semaphore_signal(ready, inc=1, device_id=other, device_id_type=MESH)

        @pl.when(c == 0)
        def _():
            pl.semaphore_wait(ready, 1)


    swap_saved = copy(saved.at[0, :, half_other], tok_s.at[mine], other)
    swap_saved.start()
    for load in small_loads:
        load.wait()
    for which in range(2):
        notes[c, which : which + 1, 0:TOK] = routes[which].astype(F32)
        notes[c, 2 + which : 3 + which, 0:TOK] = weights[which]
    swap_notes = copy(notes.at[c], notes.at[c], other)
    swap_notes.start()

    def relay_pipe(tokens, land, to_sec):
        base = count[0]
        for half in range(2):
            cp = copy(
                tokens.at[0, :, half * HALF : half * HALF + HALF],
                land.at[mine],
                (to_sec, 2 * z + half),
                sem=base + c,
            )
            cp.start()

        def wait():
            for src in range(2):
                pltpu.make_async_remote_copy(
                    src_ref=tokens.at[0, :, 0:HALF],
                    dst_ref=land.at[src * TOK : src * TOK + TOK],
                    send_sem=send_sem.at[base],
                    recv_sem=recv_sem.at[base + src],
                    device_id=other,
                    device_id_type=MESH,
                ).wait_recv()

        return wait


    def both(at):
        return jnp.concatenate([notes[0, at : at + 1, 0:TOK], notes[1, at : at + 1, 0:TOK]], axis=1)

    def slots_of(which):
        tokens = 2 * TOK
        named = jnp.broadcast_to(both(which).astype(jnp.int32), (8, tokens))
        turn = jnp.bitwise_and((named - pair) * sgn + 8, 3)
        near = jnp.where(turn == 0, 0, jnp.where(turn == 1, 2, jnp.where(turn == 2, 3, 1)))
        hot = jnp.where(near == lax.broadcasted_iota(jnp.int32, (8, tokens), 0), 1.0, 0.0)
        row = lax.broadcasted_iota(jnp.int32, (tokens, tokens), 0)
        col = lax.broadcasted_iota(jnp.int32, (tokens, tokens), 1)
        ahead = (row < col) & ((row < TOK) == (col < TOK))
        before = dot(hot.astype(BF16), jnp.where(ahead, 1.0, 0.0).astype(BF16))
        rank = jnp.sum(hot * before, axis=0, keepdims=True)
        core = jnp.where(lax.broadcasted_iota(jnp.int32, (1, tokens), 1) < TOK, 0, MOST)
        return (near[0:1] * BLOCK + core).astype(F32) + rank

    def hot_of(line):
        slots = lax.broadcasted_iota(jnp.int32, (256, 2 * TOK), 0).astype(F32)
        return jnp.where(line == slots, 1.0, 0.0)

    def make_gate(which):
        line = jnp.broadcast_to(both(2 + which), (2 * TOK, 2 * TOK))
        gates[which] = line.T

    def rows(k, n=1):
        return slice(k * BLOCK, (k + n) * BLOCK)

    def span_of(k):
        if isinstance(k, int):
            return rows(k)
        return pl.ds(pl.multiple_of(k * BLOCK, BLOCK), BLOCK)

    def arrival(src, dst, sem):
        pltpu.make_async_remote_copy(
            src_ref=src,
            dst_ref=dst,
            send_sem=send_sem.at[0],
            recv_sem=recv_sem.at[sem],
            device_id=other,
            device_id_type=MESH,
        ).wait_recv()

    class Dispatch:
        def __init__(self, tok, place, pk, rx):
            self.tok, self.place, self.pk, self.rx = tok, place, pk, rx
            self.near, self.over, self.cross = {}, {}, {}

        def send(self):
            for j in range(0, HALF, TILE):
                self.pk[:, j : j + TILE] = dot(
                    self.place[0:ROWS, :], self.tok[:, j : j + TILE]
                ).astype(BF16)
            self.rx[c, rows(0)] = self.pk[rows(0)]
            self.relay(0)
            for k in (1, 2):
                self.send_near(k)

        def send_near(self, k):
            self.near[k] = copy(self.pk.at[rows(k)], self.rx.at[c, rows(k)], target[k])
            self.near[k].start()

        def relay(self, k):
            if k:
                self.near[k].wait_recv()
            here = self.rx.at[c, rows(k)]
            self.over[k] = copy(here, self.rx.at[c, rows(4 + k)], partner)
            self.over[k].start()
            self.cross[k] = copy(here, here, other)
            self.cross[k].start()

        def hand(self, k):
            self.over[k].wait_recv()
            here = self.rx.at[c, rows(4 + k)]
            self.cross[4 + k] = copy(here, here, other)
            self.cross[4 + k].start()

        def ready(self, ks):
            for k in ks:
                self.cross[k].wait_recv()

    ds = Dispatch(tok_s, b_place, pk_s, rx_s)
    dg = Dispatch(tok_g, b_place, pk_g, rx_g)
    df = Dispatch(tok_f, f_place, pk_f, rx_f)

    def x_of(ref, chunk):
        first = chunk * ROWS
        return ref[0, first : first + ROWS, :], ref[1, first : first + ROWS, :]

    def hidden_bwd(chunk):
        @pl.loop(0, HID // TILE)
        def _(n):
            cols = pl.ds(pl.multiple_of(n * TILE, TILE), TILE)
            x0, x1 = x_of(rx_s, chunk)
            pre = dot(x0, wg[0:HALF, cols]) + dot(x1, wg[HALF:D, cols])
            up = dot(x0, wu[0:HALF, cols]) + dot(x1, wu[HALF:D, cols])
            g0, g1 = x_of(rx_g, chunk)
            back = dot(g0, wd[cols, 0:HALF], NT) + dot(g1, wd[cols, HALF:D], NT)
            sig = lax.logistic(pre)
            hid_b[:, cols] = (back * pre * sig).astype(BF16)
            hid_a[:, cols] = (back * up * sig * (1.0 + pre * (1.0 - sig))).astype(BF16)

    def hidden_fwd(chunk):
        @pl.loop(0, HID // TILE)
        def _(n):
            cols = pl.ds(pl.multiple_of(n * TILE, TILE), TILE)
            x0, x1 = x_of(rx_f, chunk)
            pre = dot(x0, wg[0:HALF, cols]) + dot(x1, wg[HALF:D, cols])
            up = dot(x0, wu[0:HALF, cols]) + dot(x1, wu[HALF:D, cols])
            hid_a[:, cols] = (pre * lax.logistic(pre) * up).astype(BF16)

    def out_bwd(half, into):
        @pl.loop(0, HALF // TILE)
        def _(j):
            at = pl.ds(pl.multiple_of(half * HALF + j * TILE, TILE), TILE)
            got = dot(hid_a[...], wg[at, :], NT) + dot(hid_b[...], wu[at, :], NT)
            into[:, pl.ds(pl.multiple_of(j * TILE, TILE), TILE)] = got.astype(into.dtype)

    def out_fwd(half, into):
        @pl.loop(0, HALF // TILE)
        def _(j):
            at = pl.ds(pl.multiple_of(half * HALF + j * TILE, TILE), TILE)
            got = dot(hid_a[...], wd[:, at])
            into[:, pl.ds(pl.multiple_of(j * TILE, TILE), TILE)] = got.astype(into.dtype)

    class Return:
        def __init__(self, hidden, out, psend, precv, own, far, pr, home, ret, pick, tok, which, result, spans, far_order):
            self.hidden, self.out = hidden, out
            self.psend, self.precv, self.own = psend, precv, own
            self.far, self.pr, self.home, self.ret = far, pr, home, ret
            self.pick, self.tok, self.which, self.result = pick, tok, which, result
            self.part, self.over, self.back, self.last = {}, {}, {}, []
            self.spans, self.far_order = spans, far_order

        def give(self, chunk):
            self.out(1 - c, self.psend.at[chunk])
            self.part[chunk] = copy(self.psend.at[chunk], self.precv.at[chunk], other)
            self.part[chunk].start()

        def keep(self, chunk):
            self.out(c, self.own.at[chunk])

        def send_far(self):
            self.part[1].wait_recv()
            for n, cols in enumerate(self.spans):
                base = count[0]
                for k in (*self.far_order, 0):
                    at = span_of(k)
                    self.far[at, cols] = (
                        self.own[1, at, cols] + self.precv[1, at, cols].astype(F32)
                    ).astype(BF16)
                    copy(self.far.at[at, cols], self.pr.at[at, cols], partner, sem=base + k).start()
                self.over[n] = base

        def sum_near(self):
            self.part[0].wait_recv()

        def send_home(self, k, n=0):
            cols = self.spans[n]
            at = span_of(k)
            arrival(self.far.at[at, cols], self.pr.at[at, cols], self.over[n] + k)
            total = (
                self.own[0, at, cols]
                + self.precv[0, at, cols].astype(F32)
                + self.pr[at, cols].astype(F32)
            ).astype(BF16)
            if isinstance(k, int) and k == 0:
                self.ret[at, cols] = total
            else:
                self.home[at, cols] = total
                if n not in self.back:
                    self.back[n] = count[0]
                    count[0] += 3
                copy(
                    self.home.at[at, cols],
                    self.ret.at[at, cols],
                    along(-k),
                    sem=self.back[n] + k - 1,
                ).start()

        def finish(self, n=0):
            for k in (1, 2, 3):
                at = span_of(k)
                arrival(self.home.at[at, self.spans[n]], self.ret.at[at, self.spans[n]], self.back[n] + k - 1)
            gate = gates[self.which]
            gate = jnp.concatenate([gate, gate], axis=1)
            theirs = pl.ds(pl.multiple_of((1 - c) * TOK, TOK), TOK)
            span = self.spans[n]
            width = span.stop - span.start

            @pl.loop(span.start // TILE, span.stop // TILE)
            def _(j):
                cols = pl.ds(pl.multiple_of(j * TILE, TILE), TILE)
                value = dot(self.pick[...], self.ret[:, cols])
                full = (self.tok[:, cols].astype(F32) + gate * value).astype(BF16)
                outs_send[self.which, :, cols] = full

            land = pl.ds(pl.multiple_of(c * HALF + span.start, TILE), width)
            part = copy(outs_send.at[self.which, theirs, span], self.result.at[0, :, land], other)
            part.start()
            self.last.append(part)
            self.result[0, :, land] = outs_send[self.which, mine, span]

        def close(self):
            for part in self.last:
                part.wait_recv()

    rb = Return(
        hidden_bwd, out_bwd, b_psend, b_precv, b_own, b_far, b_pr, b_home, b_ret, b_pick, tok_g, 1, b_out, WHOLE, (3, 2, 1)
    )
    rf = Return(
        hidden_fwd, out_fwd, f_psend, f_precv, f_own, f_far, f_pr, f_home, f_ret, f_pick, tok_f, 0, f_out, WHOLE, order_at(z + sgn)
    )

    swap_notes.wait_recv()
    b_line = slots_of(1)
    b_place[...] = hot_of(b_line).astype(BF16)
    own_saved.wait()
    swap_saved.wait_recv()
    ds.send()
    sections_ready()
    wait_g = relay_pipe(grads, tok_g, prv)
    wait_f = relay_pipe(acts, tok_f, nxt)
    f_line = slots_of(0)
    f_place[...] = hot_of(f_line).astype(BF16)
    b_pick[...] = hot_of(b_line).T.astype(BF16)
    f_pick[...] = hot_of(f_line).T.astype(BF16)
    make_gate(0)
    make_gate(1)
    f_ret[ROWS:, :] = jnp.zeros((256 - ROWS, HALF), BF16)
    b_ret[ROWS:, :] = jnp.zeros((256 - ROWS, HALF), BF16)
    ds.relay(1)
    ds.send_near(3)
    wait_g()
    dg.send()
    dg.send_near(3)
    ds.relay(2)
    ds.relay(3)
    dg.relay(1)
    wait_f()
    df.send()
    df.send_near(3)
    dg.relay(2)
    dg.relay(3)
    for k in range(4):
        ds.hand(k)
    df.relay(1)
    dg.hand(0)
    df.relay(2)
    dg.hand(1)
    df.relay(3)
    dg.hand(2)
    dg.hand(3)
    for load in loads:
        load.wait()
    ds.ready(range(4, 8))
    dg.ready(range(4, 8))
    rb.hidden(1)
    rb.give(1)
    rb.keep(1)
    rb.send_far()
    ds.ready(range(4))
    dg.ready(range(4))
    rb.hidden(0)
    for k in range(4):
        df.hand(k)
    rb.give(0)
    rb.keep(0)
    rb.sum_near()
    df.ready(range(4, 8))
    rf.hidden(1)
    rb.send_home(3)
    rf.give(1)
    rb.send_home(2)
    rf.keep(1)
    rb.send_home(1)
    rf.send_far()
    rb.send_home(0)
    df.ready(range(4))
    rf.hidden(0)
    rf.give(0)
    rf.keep(0)
    rf.sum_near()
    for k in order_at(z):
        rf.send_home(k)
    rb.finish()
    rf.send_home(0)
    rb.close()
    rf.finish()
    rf.close()
    for cp in pending:
        cp.wait_send()


def hand_on(f_in, b_in, f_res, b_res, sem):
    moves = [
        pltpu.make_async_copy(f_in, f_res, sem.at[0]),
        pltpu.make_async_copy(b_in, b_res, sem.at[1]),
    ]
    for move in moves:
        move.start()
    for move in moves:
        move.wait()


def local(acts, f_route, f_gate, saved, grads, b_route, b_gate, w_gate, w_up, w_down):
    small = [v.reshape(1, TOK) for v in (f_route, f_gate, b_route, b_gate)]
    args = (acts, *small[:2], saved, grads, *small[2:], w_gate, w_up, w_down)
    vmem = pl.BlockSpec(memory_space=pltpu.VMEM)
    hbm = pl.BlockSpec(memory_space=pl.ANY)
    tok = pltpu.VMEM((2 * TOK, HALF), BF16)
    block = pltpu.VMEM((ROWS, HALF), BF16)
    two = pltpu.VMEM((2, ROWS, HALF), BF16)
    held = pltpu.VMEM((2, 2 * ROWS, HALF), BF16)
    own = pltpu.VMEM((2, ROWS, HALF), F32)
    ret = pltpu.VMEM((256, HALF), BF16)
    stream = [two, two, own, block, block, block, ret]
    shape = jax.ShapeDtypeStruct((1, TOK, D), BF16)
    got = pl.pallas_call(
        kernel,
        out_shape=(pltpu.VMEM((1, TOK, D), BF16),) * 2,
        in_specs=[hbm] * 10,
        out_specs=(vmem, vmem),
        scratch_shapes=[
            pltpu.VMEM((D, HID), BF16),
            pltpu.VMEM((D, HID), BF16),
            pltpu.VMEM((HID, D), BF16),
            pltpu.VMEM((2, 1, TOK), jnp.int32),
            pltpu.VMEM((2, 1, TOK), F32),
            pltpu.VMEM((2, 8, 2 * TOK), F32),
            pltpu.VMEM((2, 2 * TOK, 2 * TOK), F32),
            pltpu.VMEM((256, 2 * TOK), BF16),
            pltpu.VMEM((256, 2 * TOK), BF16),
            pltpu.VMEM((2 * TOK, 256), BF16),
            pltpu.VMEM((2 * TOK, 256), BF16),
            tok,
            tok,
            tok,
            block,
            block,
            block,
            held,
            held,
            held,
            pltpu.VMEM((ROWS, HID), BF16),
            pltpu.VMEM((ROWS, HID), BF16),
            *stream,
            *stream,
            pltpu.VMEM((2, 2 * TOK, HALF), BF16),
            pltpu.SemaphoreType.DMA((N_SEM,)),
            pltpu.SemaphoreType.DMA((N_SEM,)),
            pltpu.SemaphoreType.DMA((8,)),
            pltpu.SemaphoreType.REGULAR,
        ],
        compiler_params=pltpu.CompilerParams(
            collective_id=0, has_side_effects=True, vmem_limit_bytes=56 * 2**20
        ),
        cost_estimate=pl.CostEstimate(
            flops=16 * 2 * ROWS * D * HID, bytes_accessed=14 * 2**20, transcendentals=4 * ROWS * HID
        ),
    )(*args)
    return pl.pallas_call(
        hand_on,
        out_shape=(shape, shape),
        in_specs=[vmem, vmem],
        out_specs=(hbm, hbm),
        scratch_shapes=[pltpu.SemaphoreType.DMA((2,))],
    )(*(pltpu.with_memory_space_constraint(v, pltpu.VMEM) for v in got))


def solution(mesh):
    row = P("pipe", "expert", None)
    col = P("pipe", None, "expert")
    return jax.shard_map(
        local,
        mesh=mesh,
        in_specs=(row,) * 7 + (col, col, row),
        out_specs=(row, row),
        check_vma=False,
    )
```

```python
import functools

import jax
import jax.numpy as jnp
from jax import lax
from jax.experimental import pallas as pl
from jax.experimental.pallas import tpu as pltpu
from jax.sharding import PartitionSpec as P

D = 3584
HALF = D // 2
TOK = 64
HID = 512
MOST = 24
BLOCK = 2 * MOST
ROWS = 4 * BLOCK
TILE = 256
MESH = pl.DeviceIdType.MESH
F32 = jnp.float32
BF16 = jnp.bfloat16
NN = (((1,), (0,)), ((), ()))
NT = (((1,), (1,)), ((), ()))

N_SEM = 128
WHOLE = (slice(0, HALF),)
PARTS = (slice(0, 4 * TILE), slice(4 * TILE, HALF))


def dot(a, b, how=NN):
    return lax.dot_general(a, b, how, preferred_element_type=F32)


def kernel(
    acts,
    f_route,
    f_gate,
    saved,
    grads,
    b_route,
    b_gate,
    w_gate,
    w_up,
    w_down,
    f_out,
    b_out,
    wg,
    wu,
    wd,
    routes,
    weights,
    notes,
    gates,
    f_place,
    b_place,
    f_pick,
    b_pick,
    tok_s,
    tok_g,
    tok_f,
    pk_s,
    pk_g,
    pk_f,
    rx_s,
    rx_g,
    rx_f,
    hid_a,
    hid_b,
    b_psend,
    b_precv,
    b_own,
    b_far,
    b_pr,
    b_home,
    b_ret,
    f_psend,
    f_precv,
    f_own,
    f_far,
    f_pr,
    f_home,
    f_ret,
    outs_send,
    send_sem,
    recv_sem,
    load_sem,
    ready,
):
    sec = lax.axis_index("pipe")
    ex = lax.axis_index("expert")
    n_sec = lax.axis_size("pipe")
    n_ex = lax.axis_size("expert")
    z = lax.div(ex, 2)
    c = lax.rem(ex, 2)
    sgn = 1 - 2 * lax.rem(z, 2)
    pair = lax.div(z, 2)

    def along(dist):
        return (sec, lax.rem(ex + 2 * dist * sgn + 2 * n_ex, n_ex))

    other = (sec, ex + 1 - 2 * c)
    partner = along(1)
    target = {1: along(-1), 2: along(2), 3: along(-3)}
    source = {1: along(-1), 2: along(-2), 3: along(-3)}
    nxt = lax.rem(sec + 1, n_sec)
    prv = lax.rem(sec + n_sec - 1, n_sec)

    def order_at(chip):
        second, eighth = jnp.where(chip == 2, 1, 0), jnp.where(chip == 7, 1, 0)
        return 3 - second - 2 * eighth, 2 - second, 1 + 2 * (second + eighth)

    count = [0]
    pending = []

    def copy(src, dst, to, sem=None):
        i = count[0]
        count[0] += 1
        out = pltpu.make_async_remote_copy(
            src_ref=src,
            dst_ref=dst,
            send_sem=send_sem.at[i],
            recv_sem=recv_sem.at[i] if sem is None else recv_sem.at[sem],
            device_id=to,
            device_id_type=MESH,
        )
        pending.append(out)
        return out

    loads = [
        pltpu.make_async_copy(w_gate.at[0], wg, load_sem.at[0]),
        pltpu.make_async_copy(w_up.at[0], wu, load_sem.at[1]),
        pltpu.make_async_copy(w_down.at[0], wd, load_sem.at[2]),
    ]
    mine = pl.ds(pl.multiple_of(c * TOK, TOK), TOK)
    half_mine = pl.ds(pl.multiple_of(c * HALF, HALF), HALF)
    half_other = pl.ds(pl.multiple_of((1 - c) * HALF, HALF), HALF)
    own_saved = pltpu.make_async_copy(
        saved.at[0, :, half_mine], tok_s.at[mine], load_sem.at[3]
    )
    small = ((routes, (f_route, b_route)), (weights, (f_gate, b_gate)))
    small_loads = []
    for which in (1, 0):
        for kind, (held, given) in enumerate(small):
            at = load_sem.at[4 + 2 * which + kind]
            small_loads.append(pltpu.make_async_copy(given[which], held.at[which], at))

    barrier = pltpu.get_barrier_semaphore()
    for dist in (1, -1, 2, -2, -3):
        there = along(dist)
        pl.semaphore_signal(
            barrier, inc=1, device_id=(there[0], there[1] - c), device_id_type=MESH
        )

    @pl.when(c == 1)
    def _():
        pl.semaphore_signal(barrier, inc=1, device_id=other, device_id_type=MESH)

    for there in (nxt, prv):
        pl.semaphore_signal(barrier, inc=1, device_id=(there, 2 * z + 1), device_id_type=MESH)
    for load in (*small_loads, own_saved, *loads):
        load.start()

    @pl.when(c == 0)
    def _():
        pl.semaphore_wait(barrier, 11)
        pl.semaphore_signal(ready, inc=1, device_id=other, device_id_type=MESH)

    @pl.when(c == 1)
    def _():
        pl.semaphore_wait(ready, 1)

    def sections_ready():
        @pl.when(c == 1)
        def _():
            pl.semaphore_wait(barrier, 4)
            pl.semaphore_signal(ready, inc=1, device_id=other, device_id_type=MESH)

        @pl.when(c == 0)
        def _():
            pl.semaphore_wait(ready, 1)


    swap_saved = copy(saved.at[0, :, half_other], tok_s.at[mine], other)
    swap_saved.start()
    for load in small_loads:
        load.wait()
    for which in range(2):
        notes[c, which : which + 1, 0:TOK] = routes[which].astype(F32)
        notes[c, 2 + which : 3 + which, 0:TOK] = weights[which]
    swap_notes = copy(notes.at[c], notes.at[c], other)
    swap_notes.start()

    def relay_pipe(tokens, land, to_sec):
        base = count[0]
        for half in range(2):
            cp = copy(
                tokens.at[0, :, half * HALF : half * HALF + HALF],
                land.at[mine],
                (to_sec, 2 * z + half),
                sem=base + c,
            )
            cp.start()

        def wait():
            for src in range(2):
                pltpu.make_async_remote_copy(
                    src_ref=tokens.at[0, :, 0:HALF],
                    dst_ref=land.at[src * TOK : src * TOK + TOK],
                    send_sem=send_sem.at[base],
                    recv_sem=recv_sem.at[base + src],
                    device_id=other,
                    device_id_type=MESH,
                ).wait_recv()

        return wait


    def both(at):
        return jnp.concatenate([notes[0, at : at + 1, 0:TOK], notes[1, at : at + 1, 0:TOK]], axis=1)

    def slots_of(which):
        tokens = 2 * TOK
        named = jnp.broadcast_to(both(which).astype(jnp.int32), (8, tokens))
        turn = jnp.bitwise_and((named - pair) * sgn + 8, 3)
        near = jnp.where(turn == 0, 0, jnp.where(turn == 1, 2, jnp.where(turn == 2, 3, 1)))
        hot = jnp.where(near == lax.broadcasted_iota(jnp.int32, (8, tokens), 0), 1.0, 0.0)
        row = lax.broadcasted_iota(jnp.int32, (tokens, tokens), 0)
        col = lax.broadcasted_iota(jnp.int32, (tokens, tokens), 1)
        ahead = (row < col) & ((row < TOK) == (col < TOK))
        before = dot(hot.astype(BF16), jnp.where(ahead, 1.0, 0.0).astype(BF16))
        rank = jnp.sum(hot * before, axis=0, keepdims=True)
        core = jnp.where(lax.broadcasted_iota(jnp.int32, (1, tokens), 1) < TOK, 0, MOST)
        return (near[0:1] * BLOCK + core).astype(F32) + rank

    def hot_of(line):
        slots = lax.broadcasted_iota(jnp.int32, (256, 2 * TOK), 0).astype(F32)
        return jnp.where(line == slots, 1.0, 0.0)

    def make_gate(which):
        line = jnp.broadcast_to(both(2 + which), (2 * TOK, 2 * TOK))
        gates[which] = line.T

    def rows(k, n=1):
        return slice(k * BLOCK, (k + n) * BLOCK)

    def span_of(k):
        if isinstance(k, int):
            return rows(k)
        return pl.ds(pl.multiple_of(k * BLOCK, BLOCK), BLOCK)

    def arrival(src, dst, sem):
        pltpu.make_async_remote_copy(
            src_ref=src,
            dst_ref=dst,
            send_sem=send_sem.at[0],
            recv_sem=recv_sem.at[sem],
            device_id=other,
            device_id_type=MESH,
        ).wait_recv()

    class Dispatch:
        def __init__(self, tok, place, pk, rx):
            self.tok, self.place, self.pk, self.rx = tok, place, pk, rx
            self.near, self.over, self.cross = {}, {}, {}

        def send(self):
            for j in range(0, HALF, TILE):
                self.pk[:, j : j + TILE] = dot(
                    self.place[0:ROWS, :], self.tok[:, j : j + TILE]
                ).astype(BF16)
            self.rx[c, rows(0)] = self.pk[rows(0)]
            self.relay(0)
            for k in (1, 2):
                self.send_near(k)

        def send_near(self, k):
            self.near[k] = copy(self.pk.at[rows(k)], self.rx.at[c, rows(k)], target[k])
            self.near[k].start()

        def relay(self, k):
            if k:
                self.near[k].wait_recv()
            here = self.rx.at[c, rows(k)]
            self.over[k] = copy(here, self.rx.at[c, rows(4 + k)], partner)
            self.over[k].start()
            self.cross[k] = copy(here, here, other)
            self.cross[k].start()

        def hand(self, k):
            self.over[k].wait_recv()
            here = self.rx.at[c, rows(4 + k)]
            self.cross[4 + k] = copy(here, here, other)
            self.cross[4 + k].start()

        def ready(self, ks):
            for k in ks:
                self.cross[k].wait_recv()

    ds = Dispatch(tok_s, b_place, pk_s, rx_s)
    dg = Dispatch(tok_g, b_place, pk_g, rx_g)
    df = Dispatch(tok_f, f_place, pk_f, rx_f)

    def x_of(ref, chunk):
        first = chunk * ROWS
        return ref[0, first : first + ROWS, :], ref[1, first : first + ROWS, :]

    def hidden_bwd(chunk):
        @pl.loop(0, HID // TILE)
        def _(n):
            cols = pl.ds(pl.multiple_of(n * TILE, TILE), TILE)
            x0, x1 = x_of(rx_s, chunk)
            pre = dot(x0, wg[0:HALF, cols]) + dot(x1, wg[HALF:D, cols])
            up = dot(x0, wu[0:HALF, cols]) + dot(x1, wu[HALF:D, cols])
            g0, g1 = x_of(rx_g, chunk)
            back = dot(g0, wd[cols, 0:HALF], NT) + dot(g1, wd[cols, HALF:D], NT)
            sig = lax.logistic(pre)
            hid_b[:, cols] = (back * pre * sig).astype(BF16)
            hid_a[:, cols] = (back * up * sig * (1.0 + pre * (1.0 - sig))).astype(BF16)

    def hidden_fwd(chunk):
        @pl.loop(0, HID // TILE)
        def _(n):
            cols = pl.ds(pl.multiple_of(n * TILE, TILE), TILE)
            x0, x1 = x_of(rx_f, chunk)
            pre = dot(x0, wg[0:HALF, cols]) + dot(x1, wg[HALF:D, cols])
            up = dot(x0, wu[0:HALF, cols]) + dot(x1, wu[HALF:D, cols])
            hid_a[:, cols] = (pre * lax.logistic(pre) * up).astype(BF16)

    def out_bwd(half, into):
        @pl.loop(0, HALF // TILE)
        def _(j):
            at = pl.ds(pl.multiple_of(half * HALF + j * TILE, TILE), TILE)
            got = dot(hid_a[...], wg[at, :], NT) + dot(hid_b[...], wu[at, :], NT)
            into[:, pl.ds(pl.multiple_of(j * TILE, TILE), TILE)] = got.astype(into.dtype)

    def out_fwd(half, into):
        @pl.loop(0, HALF // TILE)
        def _(j):
            at = pl.ds(pl.multiple_of(half * HALF + j * TILE, TILE), TILE)
            got = dot(hid_a[...], wd[:, at])
            into[:, pl.ds(pl.multiple_of(j * TILE, TILE), TILE)] = got.astype(into.dtype)

    class Return:
        def __init__(self, hidden, out, psend, precv, own, far, pr, home, ret, pick, tok, which, result, spans, far_order):
            self.hidden, self.out = hidden, out
            self.psend, self.precv, self.own = psend, precv, own
            self.far, self.pr, self.home, self.ret = far, pr, home, ret
            self.pick, self.tok, self.which, self.result = pick, tok, which, result
            self.part, self.over, self.back, self.last = {}, {}, {}, []
            self.spans, self.far_order = spans, far_order

        def give(self, chunk):
            self.out(1 - c, self.psend.at[chunk])
            self.part[chunk] = copy(self.psend.at[chunk], self.precv.at[chunk], other)
            self.part[chunk].start()

        def keep(self, chunk):
            self.out(c, self.own.at[chunk])

        def send_far(self):
            self.part[1].wait_recv()
            for n, cols in enumerate(self.spans):
                base = count[0]
                for k in (*self.far_order, 0):
                    at = span_of(k)
                    self.far[at, cols] = (
                        self.own[1, at, cols] + self.precv[1, at, cols].astype(F32)
                    ).astype(BF16)
                    copy(self.far.at[at, cols], self.pr.at[at, cols], partner, sem=base + k).start()
                self.over[n] = base

        def sum_near(self):
            self.part[0].wait_recv()

        def send_home(self, k, n=0):
            cols = self.spans[n]
            at = span_of(k)
            arrival(self.far.at[at, cols], self.pr.at[at, cols], self.over[n] + k)
            total = (
                self.own[0, at, cols]
                + self.precv[0, at, cols].astype(F32)
                + self.pr[at, cols].astype(F32)
            ).astype(BF16)
            if isinstance(k, int) and k == 0:
                self.ret[at, cols] = total
            else:
                self.home[at, cols] = total
                if n not in self.back:
                    self.back[n] = count[0]
                    count[0] += 3
                copy(
                    self.home.at[at, cols],
                    self.ret.at[at, cols],
                    along(-k),
                    sem=self.back[n] + k - 1,
                ).start()

        def finish(self, n=0):
            for k in (1, 2, 3):
                at = span_of(k)
                arrival(self.home.at[at, self.spans[n]], self.ret.at[at, self.spans[n]], self.back[n] + k - 1)
            gate = gates[self.which]
            gate = jnp.concatenate([gate, gate], axis=1)
            theirs = pl.ds(pl.multiple_of((1 - c) * TOK, TOK), TOK)
            span = self.spans[n]
            width = span.stop - span.start

            @pl.loop(span.start // TILE, span.stop // TILE)
            def _(j):
                cols = pl.ds(pl.multiple_of(j * TILE, TILE), TILE)
                value = dot(self.pick[...], self.ret[:, cols])
                full = (self.tok[:, cols].astype(F32) + gate * value).astype(BF16)
                outs_send[self.which, :, cols] = full

            land = pl.ds(pl.multiple_of(c * HALF + span.start, TILE), width)
            part = copy(outs_send.at[self.which, theirs, span], self.result.at[0, :, land], other)
            part.start()
            self.last.append(part)
            self.result[0, :, land] = outs_send[self.which, mine, span]

        def close(self):
            for part in self.last:
                part.wait_recv()

    rb = Return(
        hidden_bwd, out_bwd, b_psend, b_precv, b_own, b_far, b_pr, b_home, b_ret, b_pick, tok_g, 1, b_out, WHOLE, (3, 2, 1)
    )
    rf = Return(
        hidden_fwd, out_fwd, f_psend, f_precv, f_own, f_far, f_pr, f_home, f_ret, f_pick, tok_f, 0, f_out, WHOLE, order_at(z + sgn)
    )

    swap_notes.wait_recv()
    b_line = slots_of(1)
    b_place[...] = hot_of(b_line).astype(BF16)
    own_saved.wait()
    swap_saved.wait_recv()
    ds.send()
    sections_ready()
    wait_g = relay_pipe(grads, tok_g, prv)
    wait_f = relay_pipe(acts, tok_f, nxt)
    f_line = slots_of(0)
    f_place[...] = hot_of(f_line).astype(BF16)
    b_pick[...] = hot_of(b_line).T.astype(BF16)
    f_pick[...] = hot_of(f_line).T.astype(BF16)
    make_gate(0)
    make_gate(1)
    f_ret[ROWS:, :] = jnp.zeros((256 - ROWS, HALF), BF16)
    b_ret[ROWS:, :] = jnp.zeros((256 - ROWS, HALF), BF16)
    ds.relay(1)
    ds.send_near(3)
    wait_g()
    dg.send()
    dg.send_near(3)
    ds.relay(2)
    ds.relay(3)
    dg.relay(1)
    wait_f()
    df.send()
    df.send_near(3)
    dg.relay(2)
    dg.relay(3)
    for k in range(4):
        ds.hand(k)
    df.relay(1)
    dg.hand(0)
    df.relay(2)
    dg.hand(1)
    df.relay(3)
    dg.hand(2)
    dg.hand(3)
    for load in loads:
        load.wait()
    ds.ready(range(4, 8))
    dg.ready(range(4, 8))
    rb.hidden(1)
    rb.give(1)
    rb.keep(1)
    rb.send_far()
    ds.ready(range(4))
    dg.ready(range(4))
    rb.hidden(0)
    for k in range(4):
        df.hand(k)
    rb.give(0)
    rb.keep(0)
    rb.sum_near()
    df.ready(range(4, 8))
    rf.hidden(1)
    rb.send_home(3)
    rf.give(1)
    rb.send_home(2)
    rf.keep(1)
    early = len(pending)
    rf.send_far()
    rb.send_home(1)
    rb.send_home(0)
    df.ready(range(4))
    rf.hidden(0)
    rf.give(0)
    rf.keep(0)
    rf.sum_near()
    for k in order_at(z):
        rf.send_home(k)
    rb.finish()
    for cp in pending[:early]:
        cp.wait_send()
    rf.send_home(0)
    rb.close()
    rf.finish()
    rf.close()
    for cp in pending[early:]:
        cp.wait_send()


def hand_on(f_in, b_in, f_res, b_res, sem):
    moves = [
        pltpu.make_async_copy(f_in, f_res, sem.at[0]),
        pltpu.make_async_copy(b_in, b_res, sem.at[1]),
    ]
    for move in moves:
        move.start()
    for move in moves:
        move.wait()


def local(acts, f_route, f_gate, saved, grads, b_route, b_gate, w_gate, w_up, w_down):
    small = [v.reshape(1, TOK) for v in (f_route, f_gate, b_route, b_gate)]
    args = (acts, *small[:2], saved, grads, *small[2:], w_gate, w_up, w_down)
    vmem = pl.BlockSpec(memory_space=pltpu.VMEM)
    hbm = pl.BlockSpec(memory_space=pl.ANY)
    tok = pltpu.VMEM((2 * TOK, HALF), BF16)
    block = pltpu.VMEM((ROWS, HALF), BF16)
    two = pltpu.VMEM((2, ROWS, HALF), BF16)
    held = pltpu.VMEM((2, 2 * ROWS, HALF), BF16)
    own = pltpu.VMEM((2, ROWS, HALF), F32)
    ret = pltpu.VMEM((256, HALF), BF16)
    stream = [two, two, own, block, block, block, ret]
    shape = jax.ShapeDtypeStruct((1, TOK, D), BF16)
    got = pl.pallas_call(
        kernel,
        out_shape=(pltpu.VMEM((1, TOK, D), BF16),) * 2,
        in_specs=[hbm] * 10,
        out_specs=(vmem, vmem),
        scratch_shapes=[
            pltpu.VMEM((D, HID), BF16),
            pltpu.VMEM((D, HID), BF16),
            pltpu.VMEM((HID, D), BF16),
            pltpu.VMEM((2, 1, TOK), jnp.int32),
            pltpu.VMEM((2, 1, TOK), F32),
            pltpu.VMEM((2, 8, 2 * TOK), F32),
            pltpu.VMEM((2, 2 * TOK, 2 * TOK), F32),
            pltpu.VMEM((256, 2 * TOK), BF16),
            pltpu.VMEM((256, 2 * TOK), BF16),
            pltpu.VMEM((2 * TOK, 256), BF16),
            pltpu.VMEM((2 * TOK, 256), BF16),
            tok,
            tok,
            tok,
            block,
            block,
            block,
            held,
            held,
            held,
            pltpu.VMEM((ROWS, HID), BF16),
            pltpu.VMEM((ROWS, HID), BF16),
            *stream,
            *stream,
            pltpu.VMEM((2, 2 * TOK, HALF), BF16),
            pltpu.SemaphoreType.DMA((N_SEM,)),
            pltpu.SemaphoreType.DMA((N_SEM,)),
            pltpu.SemaphoreType.DMA((8,)),
            pltpu.SemaphoreType.REGULAR,
        ],
        compiler_params=pltpu.CompilerParams(
            collective_id=0, has_side_effects=True, vmem_limit_bytes=56 * 2**20
        ),
        cost_estimate=pl.CostEstimate(
            flops=16 * 2 * ROWS * D * HID, bytes_accessed=14 * 2**20, transcendentals=4 * ROWS * HID
        ),
    )(*args)
    return pl.pallas_call(
        hand_on,
        out_shape=(shape, shape),
        in_specs=[vmem, vmem],
        out_specs=(hbm, hbm),
        scratch_shapes=[pltpu.SemaphoreType.DMA((2,))],
    )(*(pltpu.with_memory_space_constraint(v, pltpu.VMEM) for v in got))


def solution(mesh):
    row = P("pipe", "expert", None)
    col = P("pipe", None, "expert")
    return jax.shard_map(
        local,
        mesh=mesh,
        in_specs=(row,) * 7 + (col, col, row),
        out_specs=(row, row),
        check_vma=False,
    )
```
